32 devices in a mesh: gx: 16 (over z, x, core), yz: 2 (over y).
Axes of the slice: x: 2, y: 2, z: 4, core: 2. Of those that a mesh axis runs over, the one named last changes fastest.
Arguments:
- conformation: float32 [3, 64, 384, 1024], P(None, 'gx', 'yz'), may hold values from -0.49 to 2.5, as said below
- velocity: float32 [3, 64, 384, 1024], P(None, 'gx', 'yz'), may hold values from -6 to 6
Outputs:
- updated: float32 [3, 64, 384, 1024], P(None, 'gx', 'yz')
The draws below stay inside these ranges and needn't reach their ends.
Inputs may be any that keep to these rules, and one draw needn't show every extreme that they name: `conformation`: components 0 and 2 (c_xx, c_yy) lie in [0.5, 2.5] and component 1 (c_xy) in [-0.49, 0.49].
All inputs are finite; a program needn't handle non-finite values.
Results may differ from the reference program's by a relative error of at most 0.000076.
Values sent between devices are 32-bit elements; how exact they have to be, the bound alone decides.
No kernel may reach another device: no remote copies, remote signals or barrier semaphores. Data moves between devices by JAX's collectives and lax.ppermute only.
A program may use at most 256 MiB of HBM per device.

```python
import math
import jax
import jax.numpy as jnp
from jax import lax

NY = 384
NZ = 1024
NX = 64
N_YZ = 2


def draw_conformation(key, part):
    first_key, second_key = jax.random.split(key, 2)
    diagonal = jax.random.uniform(first_key, (2, NX, NY, NZ), jnp.float32, 0.5, 2.5)
    offdiag = jax.random.uniform(second_key, (NX, NY, NZ), jnp.float32, -0.49, 0.49)
    return jnp.stack([diagonal[0], offdiag, diagonal[1]]).astype(jnp.float32)


def block_levels(rng, extent, cuts, smallest, high):
    def one(axis_at, shards_of):
        draws = jax.random.uniform(jax.random.fold_in(jax.random.fold_in(rng, 6), axis_at), (shards_of,), jnp.float32, smallest / len(cuts), high / len(cuts))
        return jnp.repeat(jnp.exp(draws), extent[axis_at] // shards_of).reshape((-1,) + (1,) * (len(extent) - axis_at - 1))

    gain = one(*cuts[0])
    for cut in cuts[1:]:
        gain = gain * one(*cut)
    return gain


def noise(own_key, shape, scale, most, cuts=(), kind=jnp.bfloat16):
    entries = scale * jax.random.normal(own_key, shape, jnp.float32)
    if cuts:
        entries = entries * block_levels(own_key, shape, cuts, -0.22, 0.18)
    return jnp.clip(entries, -most, most).astype(kind)


def setup_inputs(seed: int = 0) -> dict:
    key_list = jax.random.split(jax.random.key(seed), 3)
    conformation = draw_conformation(jax.random.fold_in(key_list[2], 71), 0)
    velocity = noise(key_list[1], (3, NX, NY, NZ), 1.0, 6.0, ((1, 16), (2, 2)), jnp.float32)
    return {"conformation": conformation, "velocity": velocity}


stencil_coeffs = (0.8, -0.2, 4.0 / 105.0, -1.0 / 280.0)
extensibility = 10.0
relax_rate = 1.0 / 0.04
courant = 0.5


def storage_points(count, groups):
    index = jnp.arange(count, dtype=jnp.int32)
    per_group = count // groups
    return ((index % per_group) * groups + index // per_group).astype(jnp.int32)


def cheb_matrix(count, points):
    last = count - 1
    half_step = math.pi / (2.0 * last)
    weights = jnp.where((points == 0) | (points == last), 2.0, 1.0).astype(jnp.float32)
    same = points[:, None] == points[None, :]
    sums = (points[:, None] + points[None, :]).astype(jnp.float32) * half_step
    diffs = (points[:, None] - points[None, :]).astype(jnp.float32) * half_step
    signs = (1 - 2 * ((points[:, None] + points[None, :]) % 2)).astype(jnp.float32)
    apart = -2.0 * jnp.sin(sums) * jnp.sin(diffs)
    safe = jnp.where(same, 1.0, apart)
    offdiag = jnp.where(same, 0.0, weights[:, None] / weights[None, :] * signs / safe)
    return offdiag - jnp.diag(jnp.sum(offdiag, axis=1))


def centered(padded, width, count, axis, spacing):
    total = jnp.zeros_like(lax.slice_in_dim(padded, width, width + count, axis=axis))
    for offset, coeff in enumerate(stencil_coeffs, start=1):
        ahead = lax.slice_in_dim(padded, width + offset, width + offset + count, axis=axis)
        behind = lax.slice_in_dim(padded, width - offset, width - offset + count, axis=axis)
        total = total + coeff * (ahead - behind)
    return total / spacing


def wall_terms(comp, vel_v, dy_comp, dy_u, dy_v):
    term_xx = -vel_v * dy_comp[0] + 2.0 * dy_u * comp[1]
    term_xy = -vel_v * dy_comp[1] + dy_u * comp[2] + dy_v * comp[1]
    term_yy = -vel_v * dy_comp[2] + 2.0 * dy_v * comp[2]
    return jnp.stack([term_xx, term_xy, term_yy])


def local_terms(comp, vel, along_x, along_z):
    peterlin = (extensibility - 2.0) / (extensibility - comp[0] - comp[2])
    grad_ux = along_x[3]
    grad_vx = along_x[4]
    term_xx = -vel[0] * along_x[0] - vel[2] * along_z[0] + 2.0 * grad_ux * comp[0] - relax_rate * (peterlin * comp[0] - 1.0)
    term_xy = -vel[0] * along_x[1] - vel[2] * along_z[1] + grad_ux * comp[1] + grad_vx * comp[0] - relax_rate * peterlin * comp[1]
    term_yy = -vel[0] * along_x[2] - vel[2] * along_z[2] + 2.0 * grad_vx * comp[1] - relax_rate * (peterlin * comp[2] - 1.0)
    return jnp.stack([term_xx, term_xy, term_yy])


def reference(conformation, velocity):
    count = conformation.shape[2]
    spacing = math.pi / (count - 1)
    points = storage_points(count, N_YZ)
    cheb = cheb_matrix(count, points)
    theta = math.pi * points.astype(jnp.float32) / (count - 1)
    step_size = courant * spacing * (jnp.sin(theta) + spacing)
    block = jnp.concatenate([conformation, velocity[0:2]], axis=0)
    padded = jnp.pad(block, ((0, 0), (4, 4), (0, 0), (0, 0)), mode="wrap")
    along_x = centered(padded, 4, block.shape[1], 1, spacing)
    padded_z = jnp.pad(conformation, ((0, 0), (0, 0), (0, 0), (4, 4)), mode="wrap")
    along_z = centered(padded_z, 4, conformation.shape[3], 3, spacing)
    along_y = jnp.einsum("ij,fxjz->fxiz", cheb, block, precision=lax.Precision.HIGHEST)
    yterms = wall_terms(conformation, velocity[1], along_y[0:3], along_y[3], along_y[4])
    other = local_terms(conformation, velocity, along_x, along_z)
    return conformation + step_size[None, None, :, None] * (other + yterms)
```

```python
import functools
import math

import jax
import jax.numpy as jnp
from jax import lax
from jax.experimental import pallas as pl
from jax.experimental.pallas import tpu as pltpu
from jax.sharding import PartitionSpec as P

stencil_coeffs = (0.8, -0.2, 4.0 / 105.0, -1.0 / 280.0)
width = 4
extensibility = 10.0
relax_rate = 1.0 / 0.04
courant = 0.5
row_block = 8
chunks = 2
vmem_bytes = 40 * 1024 * 1024


def cheb_matrix(count, points):
    last = count - 1
    half_step = math.pi / (2.0 * last)
    weights = jnp.where((points == 0) | (points == last), 2.0, 1.0).astype(jnp.float32)
    same = points[:, None] == points[None, :]
    sums = (points[:, None] + points[None, :]).astype(jnp.float32) * half_step
    diffs = (points[:, None] - points[None, :]).astype(jnp.float32) * half_step
    signs = (1 - 2 * ((points[:, None] + points[None, :]) % 2)).astype(jnp.float32)
    apart = -2.0 * jnp.sin(sums) * jnp.sin(diffs)
    safe = jnp.where(same, 1.0, apart)
    offdiag = jnp.where(same, 0.0, weights[:, None] / weights[None, :] * signs / safe)
    return offdiag - jnp.diag(jnp.sum(offdiag, axis=1))


def params():
    return pltpu.CompilerParams(vmem_limit_bytes=vmem_bytes)


def x_terms(u, c_xx, c_xy, sums):
    term_xx = 2.0 * sums[3] * c_xx - u * sums[0]
    term_xy = sums[3] * c_xy + sums[4] * c_xx - u * sums[1]
    term_yy = 2.0 * sums[4] * c_xy - u * sums[2]
    return term_xx, term_xy, term_yy


def from_after(planes, i, coeffs):
    return sum(coeffs[k - 1] * planes[i + k - width] for k in range(width - i, width + 1))


def from_before(planes, i, coeffs):
    return -sum(coeffs[k - 1] * planes[width + i - k] for k in range(i + 1, width + 1))


def inside(planes, i, coeffs):
    total = None
    for k in range(1, width):
        for at, sign in ((i + k, 1.0), (i - k, -1.0)):
            if 0 <= at < width:
                term = (sign * coeffs[k - 1]) * planes[at]
                total = term if total is None else total + term
    return total


def local_kernel(coeffs, lanes, step_ref, comp_ref, vel_ref, out_ref):
    step = step_ref[:, 0:1]
    for i in range(width):
        comp = [comp_ref[f, i] for f in range(3)]
        along_z = []
        for f in range(3):
            total = None
            for k in range(1, width + 1):
                ahead = pltpu.roll(comp[f], lanes - k, 1)
                behind = pltpu.roll(comp[f], k, 1)
                term = coeffs[k - 1] * (ahead - behind)
                total = term if total is None else total + term
            along_z.append(total)
        sums = [inside([comp_ref[f, j] for j in range(width)], i, coeffs) for f in range(3)]
        sums += [inside([vel_ref[f, j] for j in range(width)], i, coeffs) for f in range(2)]
        terms = x_terms(vel_ref[0, i], comp[0], comp[1], sums)
        peterlin = (extensibility - 2.0) / (extensibility - comp[0] - comp[2])
        rest = (1.0, 0.0, 1.0)
        w = vel_ref[2, i]
        for f in range(3):
            relax = relax_rate * (peterlin * comp[f] - rest[f])
            out_ref[f, i] = comp[f] + step * (terms[f] - w * along_z[f] - relax)


def local_part(coeffs, step, comp, vel):
    fields, planes, rows, lanes = comp.shape
    block = pl.BlockSpec((3, planes, row_block, lanes), lambda r: (0, 0, r, 0))
    return pl.pallas_call(
        functools.partial(local_kernel, coeffs, lanes),
        grid=(rows // row_block,),
        in_specs=[pl.BlockSpec((row_block, 128), lambda r: (r, 0)), block, block],
        out_specs=block,
        out_shape=jax.ShapeDtypeStruct(comp.shape, jnp.float32),
        compiler_params=params(),
        cost_estimate=pl.CostEstimate(
            flops=150 * comp.size, bytes_accessed=12 * comp.size, transcendentals=0
        ),
        name="local_part",
    )(step, comp, vel)


def wall_kernel(groups, rows, *refs):
    comp_ref, vel_ref = refs[1:3]
    received = refs[3 : 2 + groups]
    matrix_ref, acc_ref = refs[2 + groups : 4 + groups]
    out_ref = refs[4 + groups]
    back = refs[5 + groups :]
    matrix = matrix_ref[...]
    fields, slopes = [], []
    for f in range(5):
        own = comp_ref[f, 0] if f < 3 else vel_ref[f - 3, 0]
        column = jnp.concatenate([own] + [r[f, 0] for r in received], axis=0)
        high = column.astype(jnp.bfloat16)
        low = (column - high.astype(jnp.float32)).astype(jnp.bfloat16)
        stacked = jnp.concatenate([high, low, high], axis=0)
        slopes.append(jnp.dot(matrix, stacked, preferred_element_type=jnp.float32))
        fields.append(column)
    c_xy, c_yy, v = fields[1], fields[2], fields[4]
    terms = (
        2.0 * slopes[3] * c_xy - v * slopes[0],
        slopes[3] * c_yy + slopes[4] * c_xy - v * slopes[1],
        2.0 * slopes[4] * c_yy - v * slopes[2],
    )
    for f in range(3):
        out_ref[f, 0] = acc_ref[f, 0] + terms[f][0:rows]
        for g in range(1, groups):
            back[g - 1][f, 0] = terms[f][g * rows : (g + 1) * rows]


def wall_part(first, place, comp, vel, received, matrix, acc):
    groups = len(received) + 1
    rows, lanes = comp.shape[2:]
    planes = received[0].shape[1]
    columns = lanes // groups
    tile = min(columns, 256)
    tiles = columns // tile
    own = lambda p, i, s: (0, first + p, 0, s[0] * tiles + i)
    own_block = pl.BlockSpec((3, 1, rows, tile), own)
    sent = lambda p, i, s: (0, p, 0, i)
    grid_spec = pltpu.PrefetchScalarGridSpec(
        num_scalar_prefetch=1,
        grid=(planes, tiles),
        in_specs=[own_block, pl.BlockSpec((2, 1, rows, tile), own)]
        + [pl.BlockSpec((5, 1, rows, tile), sent)] * (groups - 1)
        + [pl.BlockSpec(matrix.shape, lambda p, i, s: (0, 0)), own_block],
        out_specs=[own_block] + [pl.BlockSpec((3, 1, rows, tile), sent)] * (groups - 1),
    )
    count = rows * groups
    shapes = [jax.ShapeDtypeStruct(acc.shape, jnp.float32)]
    shapes += [jax.ShapeDtypeStruct((3, planes, rows, columns), jnp.float32)] * (groups - 1)
    out = pl.pallas_call(
        functools.partial(wall_kernel, groups, rows),
        grid_spec=grid_spec,
        out_shape=shapes,
        input_output_aliases={3 + groups: 0},
        compiler_params=params(),
        cost_estimate=pl.CostEstimate(
            flops=30 * count * count * columns * planes,
            bytes_accessed=44 * count * columns * planes,
            transcendentals=0,
        ),
        name="wall_part",
    )(place, comp, vel, *received, matrix, acc)
    return out[0], out[1:]


def border_kernel(coeffs, returns, lanes, flag_ref, step_ref, comp_ref, vel_ref, received_ref, acc_ref, out_ref, *back_ref):
    tile = min(lanes, 256)

    def run(after):
        step = step_ref[:, 0:1]
        for at in range(0, lanes, tile):
            here = slice(at, at + tile)
            own = [[(comp_ref[f, i, :, here] if f < 3 else vel_ref[f - 3, i, :, here]) for i in range(width)] for f in range(5)]
            other = [[received_ref[f, i, :, here] for i in range(width)] for f in range(5)]
            to_mine, to_theirs = (from_after, from_before) if after else (from_before, from_after)
            for i in range(width):
                mine = [to_mine(other[f], i, coeffs) for f in range(5)]
                terms = x_terms(own[3][i], own[0][i], own[1][i], mine)
                for f in range(3):
                    out_ref[f, i, :, here] = acc_ref[f, i, :, here] + step * terms[f]
                if returns:
                    theirs = [to_theirs(own[f], i, coeffs) for f in range(5)]
                    returned = x_terms(other[3][i], other[0][i], other[1][i], theirs)
                    for f in range(3):
                        back_ref[0][f, i, :, here] = step * returned[f]

    pl.when(flag_ref[0] == 1)(lambda: run(True))
    pl.when(flag_ref[0] == 0)(lambda: run(False))


def border_part(returns, flags, coeffs, step, comp, vel, received, acc):
    planes, size, lanes = received.shape[1:]
    here = lambda r, s: (0, 0, s[1] + r, 0)
    block = pl.BlockSpec((3, planes, row_block, lanes), here)
    sent = lambda r, s: (0, 0, r, 0)
    grid_spec = pltpu.PrefetchScalarGridSpec(
        num_scalar_prefetch=1,
        grid=(size // row_block,),
        in_specs=[
            pl.BlockSpec((row_block, 128), lambda r, s: (s[1] + r, 0)),
            block,
            pl.BlockSpec((2, planes, row_block, lanes), here),
            pl.BlockSpec((5, planes, row_block, lanes), sent),
            block,
        ],
        out_specs=[block] + [pl.BlockSpec((3, planes, row_block, lanes), sent)] * returns,
    )
    out = pl.pallas_call(
        functools.partial(border_kernel, coeffs, returns, lanes),
        grid_spec=grid_spec,
        out_shape=[jax.ShapeDtypeStruct(acc.shape, jnp.float32)]
        + [jax.ShapeDtypeStruct((3, planes, size, lanes), jnp.float32)] * returns,
        input_output_aliases={5: 0},
        compiler_params=params(),
        cost_estimate=pl.CostEstimate(
            flops=64 * 3 * planes * size * lanes,
            bytes_accessed=4 * 19 * planes * size * lanes,
            transcendentals=0,
        ),
        name="border_part",
    )(flags, step, comp, vel, received, acc)
    return out


def add_kernel(place_ref, part_ref, acc_ref, out_ref):
    out_ref[...] = acc_ref[...] + part_ref[...]


def add_part(place, part, acc, block, grid, part_at, acc_at, name):
    grid_spec = pltpu.PrefetchScalarGridSpec(
        num_scalar_prefetch=1,
        grid=grid,
        in_specs=[pl.BlockSpec(block, part_at), pl.BlockSpec(block, acc_at)],
        out_specs=pl.BlockSpec(block, acc_at),
    )
    return pl.pallas_call(
        add_kernel,
        grid_spec=grid_spec,
        out_shape=jax.ShapeDtypeStruct(acc.shape, jnp.float32),
        input_output_aliases={2: 0},
        compiler_params=params(),
        cost_estimate=pl.CostEstimate(flops=part.size, bytes_accessed=12 * part.size, transcendentals=0),
        name=name,
    )(place, part, acc)


def add_wall(first, place, part, acc):
    fields, planes, rows, columns = part.shape
    block = (fields, 1, rows, columns)
    return add_part(
        place, part, acc, block, (planes,), lambda p, s: (0, p, 0, 0), lambda p, s: (0, first + p, 0, s[0]), "add_wall"
    )


def add_border(place, part, acc):
    fields, planes, size, lanes = part.shape
    block = (fields, planes, row_block, lanes)
    return add_part(
        place, part, acc, block, (size // row_block,), lambda r, s: (0, 0, r, 0), lambda r, s: (0, 0, s[0] + r, 0), "add_border"
    )


def shares(total, unit, parts):
    units = total // unit
    sizes = [unit * (units // parts + (k < units % parts)) for k in range(parts)]
    starts = [sum(sizes[:k]) for k in range(parts)]
    return [(at, size) for at, size in zip(starts, sizes) if size]


def shards(conformation, velocity):
    planes, rows, lanes = conformation.shape[1:]
    groups, slabs = lax.axis_size("yz"), lax.axis_size("gx")
    me, slab = lax.axis_index("yz"), lax.axis_index("gx")
    odd = (slab % 2).astype(jnp.int32)
    count = rows * groups
    columns = lanes // groups
    spacing = math.pi / (count - 1)
    coeffs = tuple(c / spacing for c in stencil_coeffs)
    half = rows // 2
    wall_cuts = shares(planes, 1, chunks)
    border_cuts = shares(half, row_block, chunks)
    near = [(i, i ^ 1) for i in range(slabs)]
    far = [(i, (i + 1 if i % 2 else i - 1) % slabs) for i in range(slabs)]

    def along_yz(x, by):
        return lax.ppermute(x, "yz", [(i, (i + by) % groups) for i in range(groups)])

    def cut(plane, n_planes, row, n_rows, lane, n_lanes):
        at = (0, plane, row, lane)
        return jnp.concatenate(
            [
                lax.dynamic_slice(conformation, at, (3, n_planes, n_rows, n_lanes)),
                lax.dynamic_slice(velocity, at, (2, n_planes, n_rows, n_lanes)),
            ],
            axis=0,
        )

    walls, borders = [], []
    for (plane, n_planes), (row, n_rows) in zip(wall_cuts, border_cuts):
        pieces = [None] * groups
        for g in range(1, groups):
            piece = cut(plane, n_planes, 0, rows, (me + g) % groups * columns, columns)
            pieces[groups - g] = along_yz(piece, g)
        walls.append(pieces[1:])
        piece = cut(0, planes, odd * half + row, n_rows, 0, lanes)
        borders.append(lax.ppermute(piece, "gx", far))
    beside = lax.ppermute(cut(0, planes, 0, rows, 0, lanes), "gx", near)

    index = jnp.arange(count, dtype=jnp.int32)
    points = index % rows * groups + (index // rows + me) % groups
    theta = math.pi * points.astype(jnp.float32) / (count - 1)
    step_size = courant * spacing * (jnp.sin(theta) + spacing)
    cheb = step_size[:, None] * cheb_matrix(count, points)
    high = lax.reduce_precision(cheb, 8, 7)
    low = lax.reduce_precision(cheb - high, 8, 7)
    matrix = jnp.concatenate([high, high, low], axis=1).astype(jnp.bfloat16)
    step = jnp.broadcast_to(step_size[:rows, None], (rows, 128))

    acc = local_part(coeffs, step, conformation, velocity)
    near_flags = jnp.stack([1 - odd, jnp.zeros_like(odd)])
    (acc,) = border_part(False, near_flags, coeffs, step, conformation, velocity, beside, acc)
    place = me.astype(jnp.int32).reshape(1)
    wall_back, border_back = [], []
    for k, ((plane, _), (row, _)) in enumerate(zip(wall_cuts, border_cuts)):
        acc, back = wall_part(plane, place, conformation, velocity, walls[k], matrix, acc)
        wall_back.append([along_yz(b, g) for g, b in enumerate(back, 1)])
        far_flags = jnp.stack([odd, ((1 - odd) * half + row) // row_block])
        acc, back = border_part(True, far_flags, coeffs, step, conformation, velocity, borders[k], acc)
        border_back.append(lax.ppermute(back, "gx", far))
    for k, ((plane, _), (row, _)) in enumerate(zip(wall_cuts, border_cuts)):
        for g, part in enumerate(wall_back[k], 1):
            source = ((me - g) % groups).astype(jnp.int32).reshape(1)
            acc = add_wall(plane, source, part, acc)
        acc = add_border(((odd * half + row) // row_block).reshape(1), border_back[k], acc)
    return acc


def solution(mesh):
    in_specs = (P(None, "gx", "yz", None), P(None, "gx", "yz", None))
    out_specs = P(None, "gx", "yz", None)
    return jax.shard_map(shards, mesh=mesh, in_specs=in_specs, out_specs=out_specs, check_vma=False)
```

```python
import functools
import math

import jax
import jax.numpy as jnp
from jax import lax
from jax.experimental import pallas as pl
from jax.experimental.pallas import tpu as pltpu
from jax.sharding import PartitionSpec as P

stencil_coeffs = (0.8, -0.2, 4.0 / 105.0, -1.0 / 280.0)
width = 4
extensibility = 10.0
relax_rate = 1.0 / 0.04
courant = 0.5
row_block = 8
wall_weights = (1, 1)
border_weights = (1, 1)
vmem_bytes = 56 * 1024 * 1024


def cheb_matrix(count, points):
    last = count - 1
    half_step = math.pi / (2.0 * last)
    weights = jnp.where((points == 0) | (points == last), 2.0, 1.0).astype(jnp.float32)
    same = points[:, None] == points[None, :]
    sums = (points[:, None] + points[None, :]).astype(jnp.float32) * half_step
    diffs = (points[:, None] - points[None, :]).astype(jnp.float32) * half_step
    signs = (1 - 2 * ((points[:, None] + points[None, :]) % 2)).astype(jnp.float32)
    apart = -2.0 * jnp.sin(sums) * jnp.sin(diffs)
    safe = jnp.where(same, 1.0, apart)
    offdiag = jnp.where(same, 0.0, weights[:, None] / weights[None, :] * signs / safe)
    return offdiag - jnp.diag(jnp.sum(offdiag, axis=1))


small = pl.CostEstimate(flops=1024, bytes_accessed=1024, transcendentals=0)


def params():
    return pltpu.CompilerParams(vmem_limit_bytes=vmem_bytes)


def x_terms(u, c_xx, c_xy, sums):
    term_xx = 2.0 * sums[3] * c_xx - u * sums[0]
    term_xy = sums[3] * c_xy + sums[4] * c_xx - u * sums[1]
    term_yy = 2.0 * sums[4] * c_xy - u * sums[2]
    return term_xx, term_xy, term_yy


def from_after(planes, i, coeffs):
    return sum(coeffs[k - 1] * planes[i + k - width] for k in range(width - i, width + 1))


def from_before(planes, i, coeffs):
    return -sum(coeffs[k - 1] * planes[width + i - k] for k in range(i + 1, width + 1))


def inside(planes, i, coeffs):
    total = None
    for k in range(1, width):
        for at, sign in ((i + k, 1.0), (i - k, -1.0)):
            if 0 <= at < width:
                term = (sign * coeffs[k - 1]) * planes[at]
                total = term if total is None else total + term
    return total


def local_kernel(coeffs, lanes, step_ref, comp_ref, vel_ref, out_ref):
    step = step_ref[:, 0:1]
    for i in range(width):
        comp = [comp_ref[f, i] for f in range(3)]
        along_z = []
        for f in range(3):
            total = None
            for k in range(1, width + 1):
                ahead = pltpu.roll(comp[f], lanes - k, 1)
                behind = pltpu.roll(comp[f], k, 1)
                term = coeffs[k - 1] * (ahead - behind)
                total = term if total is None else total + term
            along_z.append(total)
        sums = [inside([comp_ref[f, j] for j in range(width)], i, coeffs) for f in range(3)]
        sums += [inside([vel_ref[f, j] for j in range(width)], i, coeffs) for f in range(2)]
        terms = x_terms(vel_ref[0, i], comp[0], comp[1], sums)
        peterlin = (extensibility - 2.0) / (extensibility - comp[0] - comp[2])
        rest = (1.0, 0.0, 1.0)
        w = vel_ref[2, i]
        for f in range(3):
            relax = relax_rate * (peterlin * comp[f] - rest[f])
            out_ref[f, i] = comp[f] + step * (terms[f] - w * along_z[f] - relax)


def local_part(coeffs, step, comp, vel):
    fields, planes, rows, lanes = comp.shape
    block = pl.BlockSpec((3, planes, row_block, lanes), lambda r: (0, 0, r, 0))
    return pl.pallas_call(
        functools.partial(local_kernel, coeffs, lanes),
        grid=(rows // row_block,),
        in_specs=[pl.BlockSpec((row_block, 128), lambda r: (r, 0)), block, block],
        out_specs=block,
        out_shape=jax.ShapeDtypeStruct(comp.shape, jnp.float32),
        compiler_params=params(),
        cost_estimate=small,
        name="local_part",
    )(step, comp, vel)


def pack_kernel(place_ref, comp_ref, vel_ref, out_ref):
    out_ref[0:3] = comp_ref[...]
    out_ref[3:5] = vel_ref[...]


def pack(place, block, grid, source_at, sent_at, comp, vel, name):
    planes, rows, lanes = block
    shape = (5, grid[0] * planes, grid[1] * rows, grid[2] * lanes)
    grid_spec = pltpu.PrefetchScalarGridSpec(
        num_scalar_prefetch=1,
        grid=grid,
        in_specs=[pl.BlockSpec((3, *block), source_at), pl.BlockSpec((2, *block), source_at)],
        out_specs=pl.BlockSpec((5, *block), sent_at),
    )
    return pl.pallas_call(
        pack_kernel,
        grid_spec=grid_spec,
        out_shape=jax.ShapeDtypeStruct(shape, jnp.float32),
        compiler_params=params(),
        cost_estimate=small,
        name=name,
    )(place, comp, vel)


def pack_wall(first, planes, columns, place, comp, vel):
    rows = comp.shape[2]
    tile = min(columns, 256)
    tiles = columns // tile
    source_at = lambda p, r, i, s: (0, first + p, 0, s[0] * tiles + i)
    return pack(place, (1, rows, tile), (planes, 1, tiles), source_at, lambda p, r, i, s: (0, p, 0, i), comp, vel, "pack_wall")


def pack_border(row, size, half, place, comp, vel):
    planes, rows, lanes = comp.shape[1:]
    tall = math.gcd(2 * row_block, math.gcd(half, math.gcd(row, size)))
    source_at = lambda p, r, i, s: (0, 0, s[0] * (half // tall) + row // tall + r, 0)
    return pack(place, (planes, tall, lanes), (1, size // tall, 1), source_at, lambda p, r, i, s: (0, 0, r, 0), comp, vel, "pack_border")


def wall_kernel(groups, rows, *refs):
    comp_ref, vel_ref = refs[1:3]
    received = refs[3 : 2 + groups]
    matrix_ref, acc_ref = refs[2 + groups : 4 + groups]
    out_ref = refs[4 + groups]
    back = refs[5 + groups :]
    matrix = matrix_ref[...]
    fields, slopes = [], []
    for f in range(5):
        own = comp_ref[f, 0] if f < 3 else vel_ref[f - 3, 0]
        column = jnp.concatenate([own] + [r[f, 0] for r in received], axis=0)
        high = column.astype(jnp.bfloat16)
        low = (column - high.astype(jnp.float32)).astype(jnp.bfloat16)
        stacked = jnp.concatenate([high, low, high], axis=0)
        slopes.append(jnp.dot(matrix, stacked, preferred_element_type=jnp.float32))
        fields.append(column)
    c_xy, c_yy, v = fields[1], fields[2], fields[4]
    terms = (
        2.0 * slopes[3] * c_xy - v * slopes[0],
        slopes[3] * c_yy + slopes[4] * c_xy - v * slopes[1],
        2.0 * slopes[4] * c_yy - v * slopes[2],
    )
    for f in range(3):
        out_ref[f, 0] = acc_ref[f, 0] + terms[f][0:rows]
        for g in range(1, groups):
            back[g - 1][f, 0] = terms[f][g * rows : (g + 1) * rows]


def wall_part(first, place, comp, vel, received, matrix, acc):
    groups = len(received) + 1
    rows, lanes = comp.shape[2:]
    planes = received[0].shape[1]
    columns = lanes // groups
    tile = min(columns, 256)
    tiles = columns // tile
    own = lambda p, i, s: (0, first + p, 0, s[0] * tiles + i)
    own_block = pl.BlockSpec((3, 1, rows, tile), own)
    sent = lambda p, i, s: (0, p, 0, i)
    grid_spec = pltpu.PrefetchScalarGridSpec(
        num_scalar_prefetch=1,
        grid=(planes, tiles),
        in_specs=[own_block, pl.BlockSpec((2, 1, rows, tile), own)]
        + [pl.BlockSpec((5, 1, rows, tile), sent)] * (groups - 1)
        + [pl.BlockSpec(matrix.shape, lambda p, i, s: (0, 0)), own_block],
        out_specs=[own_block] + [pl.BlockSpec((3, 1, rows, tile), sent)] * (groups - 1),
    )
    count = rows * groups
    shapes = [jax.ShapeDtypeStruct(acc.shape, jnp.float32)]
    shapes += [jax.ShapeDtypeStruct((3, planes, rows, columns), jnp.float32)] * (groups - 1)
    out = pl.pallas_call(
        functools.partial(wall_kernel, groups, rows),
        grid_spec=grid_spec,
        out_shape=shapes,
        input_output_aliases={3 + groups: 0},
        compiler_params=params(),
        cost_estimate=small,
        name="wall_part",
    )(place, comp, vel, *received, matrix, acc)
    return out[0], out[1:]


def border_kernel(coeffs, returns, lanes, flag_ref, step_ref, comp_ref, vel_ref, *refs):
    received, acc_ref, out_ref, back_ref = (refs[:1], *refs[1:]) if returns else (refs[:2], *refs[2:], None)
    tile = min(lanes, 256)

    def run(after):
        step = step_ref[:, 0:1]
        for at in range(0, lanes, tile):
            here = slice(at, at + tile)
            own = [[(comp_ref[f, i, :, here] if f < 3 else vel_ref[f - 3, i, :, here]) for i in range(width)] for f in range(5)]
            fields = [(received[0], f) for f in range(5)] if returns else [(received[f // 3], f % 3) for f in range(5)]
            other = [[r[f, i, :, here] for i in range(width)] for r, f in fields]
            to_mine, to_theirs = (from_after, from_before) if after else (from_before, from_after)
            for i in range(width):
                mine = [to_mine(other[f], i, coeffs) for f in range(5)]
                terms = x_terms(own[3][i], own[0][i], own[1][i], mine)
                for f in range(3):
                    out_ref[f, i, :, here] = acc_ref[f, i, :, here] + step * terms[f]
                if returns:
                    theirs = [to_theirs(own[f], i, coeffs) for f in range(5)]
                    returned = x_terms(other[3][i], other[0][i], other[1][i], theirs)
                    for f in range(3):
                        back_ref[f, i, :, here] = step * returned[f]

    pl.when(flag_ref[0] == 1)(lambda: run(True))
    pl.when(flag_ref[0] == 0)(lambda: run(False))


def border_part(returns, flags, coeffs, step, comp, vel, received, acc):
    planes, size, lanes = received[0].shape[1:]
    here = lambda r, s: (0, 0, s[1] + r, 0)
    block = pl.BlockSpec((3, planes, row_block, lanes), here)
    sent = lambda r, s: (0, 0, r, 0)
    grid_spec = pltpu.PrefetchScalarGridSpec(
        num_scalar_prefetch=1,
        grid=(size // row_block,),
        in_specs=[
            pl.BlockSpec((row_block, 128), lambda r, s: (s[1] + r, 0)),
            block,
            pl.BlockSpec((2, planes, row_block, lanes), here),
            *(pl.BlockSpec((min(x.shape[0], 5 - at), planes, row_block, lanes), sent) for at, x in zip((0, 3), received)),
            block,
        ],
        out_specs=[block] + [pl.BlockSpec((3, planes, row_block, lanes), sent)] * returns,
    )
    out = pl.pallas_call(
        functools.partial(border_kernel, coeffs, returns, lanes),
        grid_spec=grid_spec,
        out_shape=[jax.ShapeDtypeStruct(acc.shape, jnp.float32)]
        + [jax.ShapeDtypeStruct((3, planes, size, lanes), jnp.float32)] * returns,
        input_output_aliases={4 + len(received): 0},
        compiler_params=params(),
        cost_estimate=small,
        name="border_part",
    )(flags, step, comp, vel, *received, acc)
    return out


def add_kernel(place_ref, part_ref, acc_ref, out_ref):
    out_ref[...] = acc_ref[...] + part_ref[...]


def add_part(place, part, acc, block, grid, part_at, acc_at, name):
    grid_spec = pltpu.PrefetchScalarGridSpec(
        num_scalar_prefetch=1,
        grid=grid,
        in_specs=[pl.BlockSpec(block, part_at), pl.BlockSpec(block, acc_at)],
        out_specs=pl.BlockSpec(block, acc_at),
    )
    return pl.pallas_call(
        add_kernel,
        grid_spec=grid_spec,
        out_shape=jax.ShapeDtypeStruct(acc.shape, jnp.float32),
        input_output_aliases={2: 0},
        compiler_params=params(),
        cost_estimate=small,
        name=name,
    )(place, part, acc)


def add_wall(first, place, part, acc):
    fields, planes, rows, columns = part.shape
    block = (fields, 1, rows, columns)
    return add_part(
        place, part, acc, block, (planes,), lambda p, s: (0, p, 0, 0), lambda p, s: (0, first + p, 0, s[0]), "add_wall"
    )


def add_border(row, half, place, part, acc):
    fields, planes, size, lanes = part.shape
    tall = math.gcd(2 * row_block, math.gcd(half, math.gcd(row, size)))
    block = (fields, planes, tall, lanes)
    acc_at = lambda r, s: (0, 0, s[0] * (half // tall) + row // tall + r, 0)
    return add_part(place, part, acc, block, (size // tall,), lambda r, s: (0, 0, r, 0), acc_at, "add_border")


def shares(total, unit, weights):
    units = total // unit
    ends = [unit * round(units * sum(weights[: k + 1]) / sum(weights)) for k in range(len(weights))]
    return list(zip([0] + ends[:-1], [b - a for a, b in zip([0] + ends[:-1], ends)]))


def shards(conformation, velocity):
    planes, rows, lanes = conformation.shape[1:]
    groups, slabs = lax.axis_size("yz"), lax.axis_size("gx")
    me, slab = lax.axis_index("yz"), lax.axis_index("gx")
    odd = (slab % 2).astype(jnp.int32)
    count = rows * groups
    columns = lanes // groups
    spacing = math.pi / (count - 1)
    coeffs = tuple(c / spacing for c in stencil_coeffs)
    half = rows // 2
    wall_cuts = shares(planes, 1, wall_weights)
    border_cuts = shares(half, row_block, border_weights)
    near = [(i, i ^ 1) for i in range(slabs)]
    far = [(i, (i + 1 if i % 2 else i - 1) % slabs) for i in range(slabs)]

    def along_yz(x, by):
        return lax.ppermute(x, "yz", [(i, (i + by) % groups) for i in range(groups)])

    beside = [lax.ppermute(x, "gx", near) for x in (conformation, velocity)]
    walls, borders = [], []
    for (plane, n_planes), (row, n_rows) in zip(wall_cuts, border_cuts):
        pieces = [None] * groups
        for g in range(1, groups):
            place = ((me + g) % groups).astype(jnp.int32).reshape(1)
            piece = pack_wall(plane, n_planes, columns, place, conformation, velocity)
            pieces[groups - g] = along_yz(piece, g)
        walls.append(pieces[1:])
        piece = pack_border(row, n_rows, half, odd.reshape(1), conformation, velocity)
        borders.append(lax.ppermute(piece, "gx", far))
    index = jnp.arange(count, dtype=jnp.int32)
    points = index % rows * groups + (index // rows + me) % groups
    theta = math.pi * points.astype(jnp.float32) / (count - 1)
    step_size = courant * spacing * (jnp.sin(theta) + spacing)
    cheb = step_size[:, None] * cheb_matrix(count, points)
    high = lax.reduce_precision(cheb, 8, 7)
    low = lax.reduce_precision(cheb - high, 8, 7)
    matrix = jnp.concatenate([high, high, low], axis=1).astype(jnp.bfloat16)
    step = jnp.broadcast_to(step_size[:rows, None], (rows, 128))

    acc = local_part(coeffs, step, conformation, velocity)
    near_flags = jnp.stack([1 - odd, jnp.zeros_like(odd)])
    (acc,) = border_part(False, near_flags, coeffs, step, conformation, velocity, beside, acc)
    place = me.astype(jnp.int32).reshape(1)
    wall_back, border_back = [], []
    for k, ((plane, _), (row, _)) in enumerate(zip(wall_cuts, border_cuts)):
        acc, back = wall_part(plane, place, conformation, velocity, walls[k], matrix, acc)
        wall_back.append([along_yz(b, g) for g, b in enumerate(back, 1)])
        far_flags = jnp.stack([odd, ((1 - odd) * half + row) // row_block])
        acc, back = border_part(True, far_flags, coeffs, step, conformation, velocity, [borders[k]], acc)
        border_back.append(lax.ppermute(back, "gx", far))
    for k, ((plane, _), (row, _)) in enumerate(zip(wall_cuts, border_cuts)):
        for g, part in enumerate(wall_back[k], 1):
            source = ((me - g) % groups).astype(jnp.int32).reshape(1)
            acc = add_wall(plane, source, part, acc)
        acc = add_border(row, half, odd.reshape(1), border_back[k], acc)
    return acc


def solution(mesh):
    in_specs = (P(None, "gx", "yz", None), P(None, "gx", "yz", None))
    out_specs = P(None, "gx", "yz", None)
    return jax.shard_map(shards, mesh=mesh, in_specs=in_specs, out_specs=out_specs, check_vma=False)
```

```python
import functools
import math

import jax
import jax.numpy as jnp
from jax import lax
from jax.experimental import pallas as pl
from jax.experimental.pallas import tpu as pltpu
from jax.sharding import PartitionSpec as P

stencil_coeffs = (0.8, -0.2, 4.0 / 105.0, -1.0 / 280.0)
width = 4
extensibility = 10.0
relax_rate = 1.0 / 0.04
courant = 0.5
row_block = 8
share_weights = ((1,), (2, 1))
vmem_bytes = 56 * 1024 * 1024


def cheb_matrix(count, points):
    last = count - 1
    half_step = math.pi / (2.0 * last)
    weights = jnp.where((points == 0) | (points == last), 2.0, 1.0).astype(jnp.float32)
    same = points[:, None] == points[None, :]
    sums = (points[:, None] + points[None, :]).astype(jnp.float32) * half_step
    diffs = (points[:, None] - points[None, :]).astype(jnp.float32) * half_step
    signs = (1 - 2 * ((points[:, None] + points[None, :]) % 2)).astype(jnp.float32)
    apart = -2.0 * jnp.sin(sums) * jnp.sin(diffs)
    safe = jnp.where(same, 1.0, apart)
    offdiag = jnp.where(same, 0.0, weights[:, None] / weights[None, :] * signs / safe)
    return offdiag - jnp.diag(jnp.sum(offdiag, axis=1))


small = pl.CostEstimate(flops=1024, bytes_accessed=1024, transcendentals=0)
heavy = pl.CostEstimate(flops=100000000000, bytes_accessed=1024, transcendentals=0)


def params():
    return pltpu.CompilerParams(vmem_limit_bytes=vmem_bytes)


def x_terms(u, c_xx, c_xy, sums):
    term_xx = 2.0 * sums[3] * c_xx - u * sums[0]
    term_xy = sums[3] * c_xy + sums[4] * c_xx - u * sums[1]
    term_yy = 2.0 * sums[4] * c_xy - u * sums[2]
    return term_xx, term_xy, term_yy


def from_after(planes, i, coeffs):
    return sum(coeffs[k - 1] * planes[i + k - width] for k in range(width - i, width + 1))


def from_before(planes, i, coeffs):
    return -sum(coeffs[k - 1] * planes[width + i - k] for k in range(i + 1, width + 1))


def inside(planes, i, coeffs):
    total = None
    for k in range(1, width):
        for at, sign in ((i + k, 1.0), (i - k, -1.0)):
            if 0 <= at < width:
                term = (sign * coeffs[k - 1]) * planes[at]
                total = term if total is None else total + term
    return total


def local_kernel(coeffs, lanes, step_ref, comp_ref, vel_ref, out_ref):
    step = step_ref[:, 0:1]
    for i in range(width):
        comp = [comp_ref[f, i] for f in range(3)]
        along_z = []
        for f in range(3):
            total = None
            for k in range(1, width + 1):
                ahead = pltpu.roll(comp[f], lanes - k, 1)
                behind = pltpu.roll(comp[f], k, 1)
                term = coeffs[k - 1] * (ahead - behind)
                total = term if total is None else total + term
            along_z.append(total)
        sums = [inside([comp_ref[f, j] for j in range(width)], i, coeffs) for f in range(3)]
        sums += [inside([vel_ref[f, j] for j in range(width)], i, coeffs) for f in range(2)]
        terms = x_terms(vel_ref[0, i], comp[0], comp[1], sums)
        peterlin = (extensibility - 2.0) / (extensibility - comp[0] - comp[2])
        rest = (1.0, 0.0, 1.0)
        w = vel_ref[2, i]
        for f in range(3):
            relax = relax_rate * (peterlin * comp[f] - rest[f])
            out_ref[f, i] = comp[f] + step * (terms[f] - w * along_z[f] - relax)


def pack_kernel(boxes, place_ref, comp_ref, vel_ref, *refs):
    outs, held, sems = refs[: len(boxes)], refs[len(boxes) : -1], refs[-1]
    loads, stores = [], []
    for j, (plane, n_planes, row, row_unit, n_rows, lane_unit, n_lanes) in enumerate(boxes):
        rows = pl.ds(pl.multiple_of(place_ref[j] * row_unit + row, row_block), n_rows)
        lanes = pl.ds(pl.multiple_of(place_ref[j] * lane_unit, 128), n_lanes)
        for source, first, fields in ((comp_ref, 0, 3), (vel_ref, 3, 2)):
            for f in range(fields):
                for p in range(n_planes):
                    k, to = len(loads), (first + f, p)
                    loads.append(pltpu.make_async_copy(source.at[f, plane + p, rows, lanes], held[j].at[to], sems.at[0, k]))
                    stores.append(pltpu.make_async_copy(held[j].at[to], outs[j].at[to], sems.at[1, k]))
    for load in loads:
        load.start()
    for load, store in zip(loads, stores):
        load.wait()
        store.start()
    for store in stores:
        store.wait()


def pack(places, boxes, comp, vel):
    here = pl.BlockSpec(memory_space=pltpu.HBM)
    shapes = [(5, planes, rows, lanes) for _, planes, _, _, rows, _, lanes in boxes]
    return pl.pallas_call(
        functools.partial(pack_kernel, boxes),
        in_specs=[pl.BlockSpec(memory_space=pltpu.SMEM), here, here],
        out_specs=[here] * len(boxes),
        out_shape=[jax.ShapeDtypeStruct(shape, jnp.float32) for shape in shapes],
        scratch_shapes=[pltpu.VMEM(shape, jnp.float32) for shape in shapes]
        + [pltpu.SemaphoreType.DMA((2, sum(5 * shape[1] for shape in shapes)))],
        compiler_params=params(),
        cost_estimate=small,
        name="pack",
    )(places, comp, vel)


def wall_kernel(groups, rows, *refs):
    comp_ref, vel_ref = refs[1:3]
    received = refs[3 : 2 + groups]
    matrix_ref, acc_ref = refs[2 + groups : 4 + groups]
    out_ref = refs[4 + groups]
    back = refs[5 + groups :]
    matrix = matrix_ref[...]
    fields, slopes = [], []
    for f in range(5):
        own = comp_ref[f, 0] if f < 3 else vel_ref[f - 3, 0]
        column = jnp.concatenate([own] + [r[f, 0] for r in received], axis=0)
        high = column.astype(jnp.bfloat16)
        low = (column - high.astype(jnp.float32)).astype(jnp.bfloat16)
        stacked = jnp.concatenate([high, low, high], axis=0)
        slopes.append(jnp.dot(matrix, stacked, preferred_element_type=jnp.float32))
        fields.append(column)
    c_xy, c_yy, v = fields[1], fields[2], fields[4]
    terms = (
        2.0 * slopes[3] * c_xy - v * slopes[0],
        slopes[3] * c_yy + slopes[4] * c_xy - v * slopes[1],
        2.0 * slopes[4] * c_yy - v * slopes[2],
    )
    for f in range(3):
        out_ref[f, 0] = acc_ref[f, 0] + terms[f][0:rows]
        for g in range(1, groups):
            back[g - 1][f, 0] = terms[f][g * rows : (g + 1) * rows]


def wall_part(first, skip, planes, place, comp, vel, received, matrix, acc):
    groups = len(received) + 1
    rows, lanes = comp.shape[2:]
    columns = lanes // groups
    tile = min(columns, 256)
    tiles = columns // tile
    own = lambda p, i, s: (0, first + p, 0, s[0] * tiles + i)
    own_block = pl.BlockSpec((3, 1, rows, tile), own)
    held = lambda p, i, s: (0, skip + p, 0, i)
    sent = lambda p, i, s: (0, p, 0, i)
    grid_spec = pltpu.PrefetchScalarGridSpec(
        num_scalar_prefetch=1,
        grid=(planes, tiles),
        in_specs=[own_block, pl.BlockSpec((2, 1, rows, tile), own)]
        + [pl.BlockSpec((5, 1, rows, tile), held)] * (groups - 1)
        + [pl.BlockSpec(matrix.shape, lambda p, i, s: (0, 0)), own_block],
        out_specs=[own_block] + [pl.BlockSpec((3, 1, rows, tile), sent)] * (groups - 1),
    )
    count = rows * groups
    shapes = [jax.ShapeDtypeStruct(acc.shape, jnp.float32)]
    shapes += [jax.ShapeDtypeStruct((3, planes, rows, columns), jnp.float32)] * (groups - 1)
    out = pl.pallas_call(
        functools.partial(wall_kernel, groups, rows),
        grid_spec=grid_spec,
        out_shape=shapes,
        input_output_aliases={3 + groups: 0},
        compiler_params=params(),
        cost_estimate=heavy,
        name="wall_part",
    )(place, comp, vel, *received, matrix, acc)
    return out[0], out[1:]


def border_kernel(coeffs, returns, lanes, flag_ref, step_ref, comp_ref, vel_ref, *refs):
    received, acc_ref, out_ref, back_ref = (refs[:1], *refs[1:]) if returns else (refs[:2], *refs[2:], None)
    tile = min(lanes, 256)

    def run(after):
        step = step_ref[:, 0:1]
        for at in range(0, lanes, tile):
            here = slice(at, at + tile)
            own = [[(comp_ref[f, i, :, here] if f < 3 else vel_ref[f - 3, i, :, here]) for i in range(width)] for f in range(5)]
            fields = [(received[0], f) for f in range(5)] if returns else [(received[f // 3], f % 3) for f in range(5)]
            other = [[r[f, i, :, here] for i in range(width)] for r, f in fields]
            to_mine, to_theirs = (from_after, from_before) if after else (from_before, from_after)
            for i in range(width):
                mine = [to_mine(other[f], i, coeffs) for f in range(5)]
                terms = x_terms(own[3][i], own[0][i], own[1][i], mine)
                for f in range(3):
                    out_ref[f, i, :, here] = acc_ref[f, i, :, here] + step * terms[f]
                if returns:
                    theirs = [to_theirs(own[f], i, coeffs) for f in range(5)]
                    returned = x_terms(other[3][i], other[0][i], other[1][i], theirs)
                    for f in range(3):
                        back_ref[f, i, :, here] = step * returned[f]

    pl.when(flag_ref[0] == 1)(lambda: run(True))
    pl.when(flag_ref[0] == 0)(lambda: run(False))


def border_part(returns, skip, size, flags, coeffs, step, comp, vel, received, acc):
    planes, lanes = comp.shape[1], comp.shape[3]
    here = lambda r, s: (0, 0, s[1] + r, 0)
    block = pl.BlockSpec((3, planes, row_block, lanes), here)
    held = lambda r, s: (0, 0, skip // row_block + r, 0)
    sent = lambda r, s: (0, 0, r, 0)
    grid_spec = pltpu.PrefetchScalarGridSpec(
        num_scalar_prefetch=1,
        grid=(size // row_block,),
        in_specs=[
            pl.BlockSpec((row_block, 128), lambda r, s: (s[1] + r, 0)),
            block,
            pl.BlockSpec((2, planes, row_block, lanes), here),
            *(pl.BlockSpec((min(x.shape[0], 5 - at), planes, row_block, lanes), held) for at, x in zip((0, 3), received)),
            block,
        ],
        out_specs=[block] + [pl.BlockSpec((3, planes, row_block, lanes), sent)] * returns,
    )
    out = pl.pallas_call(
        functools.partial(border_kernel, coeffs, returns, lanes),
        grid_spec=grid_spec,
        out_shape=[jax.ShapeDtypeStruct(acc.shape, jnp.float32)]
        + [jax.ShapeDtypeStruct((3, planes, size, lanes), jnp.float32)] * returns,
        input_output_aliases={4 + len(received): 0},
        compiler_params=params(),
        cost_estimate=heavy if returns else small,
        name="border_part",
    )(flags, step, comp, vel, *received, acc)
    return out


def first_kernel(coeffs, lanes, flag_ref, step_ref, comp_ref, vel_ref, comp_near, vel_near, out_ref):
    local_kernel(coeffs, lanes, step_ref, comp_ref, vel_ref, out_ref)
    border_kernel(coeffs, False, lanes, flag_ref, step_ref, comp_ref, vel_ref, comp_near, vel_near, out_ref, out_ref)


def first_part(flags, coeffs, step, comp, vel, comp_near, vel_near):
    fields, planes, rows, lanes = comp.shape
    at = lambda r, s: (0, 0, r, 0)
    block = pl.BlockSpec((fields, planes, row_block, lanes), at)
    two = pl.BlockSpec((2, planes, row_block, lanes), at)
    grid_spec = pltpu.PrefetchScalarGridSpec(
        num_scalar_prefetch=1,
        grid=(rows // row_block,),
        in_specs=[pl.BlockSpec((row_block, 128), lambda r, s: (r, 0)), block, block, block, two],
        out_specs=block,
    )
    return pl.pallas_call(
        functools.partial(first_kernel, coeffs, lanes),
        grid_spec=grid_spec,
        out_shape=jax.ShapeDtypeStruct(comp.shape, jnp.float32),
        compiler_params=params(),
        cost_estimate=small,
        name="first_part",
    )(flags, step, comp, vel, comp_near, vel_near)


def add_kernel(first, row, row_unit, lane_unit, place_ref, part_ref, acc_ref, out_ref, parts, sums, sems):
    fields, planes, size, lanes = part_ref.shape
    rows = pl.ds(pl.multiple_of(place_ref[0] * row_unit + row, row_block), size)
    columns = pl.ds(pl.multiple_of(place_ref[0] * lane_unit, 128), lanes)
    pieces = [(f, p) for f in range(fields) for p in range(planes)]
    loads, stores = [], []
    for k, (f, p) in enumerate(pieces):
        loads.append(
            (
                pltpu.make_async_copy(part_ref.at[f, p], parts.at[f, p], sems.at[0, k]),
                pltpu.make_async_copy(acc_ref.at[f, first + p, rows, columns], sums.at[f, p], sems.at[1, k]),
            )
        )
        stores.append(pltpu.make_async_copy(parts.at[f, p], out_ref.at[f, first + p, rows, columns], sems.at[2, k]))
    for pair in loads:
        for load in pair:
            load.start()
    for (f, p), pair, store in zip(pieces, loads, stores):
        for load in pair:
            load.wait()
        parts[f, p] = parts[f, p] + sums[f, p]
        store.start()
    for store in stores:
        store.wait()


def add_part(first, row, row_unit, lane_unit, place, part, acc):
    here = pl.BlockSpec(memory_space=pltpu.HBM)
    return pl.pallas_call(
        functools.partial(add_kernel, first, row, row_unit, lane_unit),
        in_specs=[pl.BlockSpec(memory_space=pltpu.SMEM), pl.BlockSpec(memory_space=pl.ANY), here],
        out_specs=here,
        out_shape=jax.ShapeDtypeStruct(acc.shape, jnp.float32),
        input_output_aliases={2: 0},
        scratch_shapes=[pltpu.VMEM(part.shape, jnp.float32)] * 2
        + [pltpu.SemaphoreType.DMA((3, part.shape[0] * part.shape[1]))],
        compiler_params=params(),
        cost_estimate=small,
        name="add_part",
    )(place, part, acc)


def shares(total, unit):
    flat = [w for share in share_weights for w in share]
    ends = [unit * round(total // unit * sum(flat[:k]) / sum(flat)) for k in range(len(flat) + 1)]
    cuts, k = [], 0
    for share in share_weights:
        own = [(a, b - a) for a, b in zip(ends[k:], ends[k + 1 : k + 1 + len(share)]) if b > a]
        cuts.append((ends[k], ends[k + len(share)] - ends[k], own))
        k += len(share)
    return [cut for cut in cuts if cut[1]]


def shards(conformation, velocity):
    planes, rows, lanes = conformation.shape[1:]
    groups, slabs = lax.axis_size("yz"), lax.axis_size("gx")
    me, slab = lax.axis_index("yz"), lax.axis_index("gx")
    odd = (slab % 2).astype(jnp.int32)
    count = rows * groups
    columns = lanes // groups
    spacing = math.pi / (count - 1)
    coeffs = tuple(c / spacing for c in stencil_coeffs)
    half = rows // 2
    wall_cuts = shares(planes, 1)
    border_cuts = shares(half, row_block)
    near = [(i, i ^ 1) for i in range(slabs)]
    far = [(i, (i + 1 if i % 2 else i - 1) % slabs) for i in range(slabs)]

    def along_yz(x, by):
        return lax.ppermute(x, "yz", [(i, (i + by) % groups) for i in range(groups)])

    beside = [lax.ppermute(x, "gx", near) for x in (conformation, velocity)]
    walls, borders = [], []
    for k in range(len(share_weights)):
        places, boxes = [], []
        for plane, n_planes, _ in wall_cuts[k : k + 1]:
            places += [(me + g) % groups for g in range(1, groups)]
            boxes += [(plane, n_planes, 0, 0, rows, columns, columns)] * (groups - 1)
        for row, n_rows, _ in border_cuts[k : k + 1]:
            places.append(odd)
            boxes.append((0, planes, row, half, n_rows, 0, lanes))
        packed = [
            pack(place.astype(jnp.int32).reshape(1), [box], conformation, velocity)[0] for place, box in zip(places, boxes)
        ]
        if k < len(wall_cuts):
            walls.append([along_yz(packed[g - 1], g) for g in range(1, groups)][::-1])
        if k < len(border_cuts):
            borders.append(lax.ppermute(packed[-1], "gx", far))

    index = jnp.arange(count, dtype=jnp.int32)
    points = index % rows * groups + (index // rows + me) % groups
    theta = math.pi * points.astype(jnp.float32) / (count - 1)
    step_size = courant * spacing * (jnp.sin(theta) + spacing)
    cheb = step_size[:, None] * cheb_matrix(count, points)
    high = lax.reduce_precision(cheb, 8, 7)
    low = lax.reduce_precision(cheb - high, 8, 7)
    matrix = jnp.concatenate([high, high, low], axis=1).astype(jnp.bfloat16)
    step = jnp.broadcast_to(step_size[:rows, None], (rows, 128))

    acc = first_part((1 - odd).reshape(1), coeffs, step, conformation, velocity, *beside)
    place = me.astype(jnp.int32).reshape(1)
    returned = []
    for k in range(len(share_weights)):
        wall_own = wall_cuts[k][2] if k < len(wall_cuts) else []
        border_own = border_cuts[k][2] if k < len(border_cuts) else []
        for j in range(max(len(wall_own), len(border_own))):
            if j < len(wall_own):
                at, size = wall_own[j]
                acc, back = wall_part(
                    at, at - wall_cuts[k][0], size, place, conformation, velocity, walls[k], matrix, acc
                )
                for g, b in enumerate(back, 1):
                    source = ((me - g) % groups).astype(jnp.int32).reshape(1)
                    returned.append((at, 0, 0, columns, source, along_yz(b, g)))
            if j < len(border_own):
                at, size = border_own[j]
                far_flags = jnp.stack([odd, ((1 - odd) * half + at) // row_block])
                acc, back = border_part(
                    True, at - border_cuts[k][0], size, far_flags, coeffs, step, conformation, velocity, [borders[k]], acc
                )
                returned.append((0, at, half, 0, odd.reshape(1), lax.ppermute(back, "gx", far)))
    for first, row, row_unit, lane_unit, source, part in returned:
        acc = add_part(first, row, row_unit, lane_unit, source, part, acc)
    return acc


def solution(mesh):
    in_specs = (P(None, "gx", "yz", None), P(None, "gx", "yz", None))
    out_specs = P(None, "gx", "yz", None)
    return jax.shard_map(shards, mesh=mesh, in_specs=in_specs, out_specs=out_specs, check_vma=False)
```

```python
import functools
import math

import jax
import jax.numpy as jnp
from jax import lax
from jax.experimental import pallas as pl
from jax.experimental.pallas import tpu as pltpu
from jax.sharding import PartitionSpec as P

stencil_coeffs = (0.8, -0.2, 4.0 / 105.0, -1.0 / 280.0)
width = 4
extensibility = 10.0
relax_rate = 1.0 / 0.04
courant = 0.5
row_block = 8
share_weights = ((3,), (7, 2))
vmem_bytes = 56 * 1024 * 1024


def cheb_matrix(count, points):
    last = count - 1
    half_step = math.pi / (2.0 * last)
    weights = jnp.where((points == 0) | (points == last), 2.0, 1.0).astype(jnp.float32)
    same = points[:, None] == points[None, :]
    sums = (points[:, None] + points[None, :]).astype(jnp.float32) * half_step
    diffs = (points[:, None] - points[None, :]).astype(jnp.float32) * half_step
    signs = (1 - 2 * ((points[:, None] + points[None, :]) % 2)).astype(jnp.float32)
    apart = -2.0 * jnp.sin(sums) * jnp.sin(diffs)
    safe = jnp.where(same, 1.0, apart)
    offdiag = jnp.where(same, 0.0, weights[:, None] / weights[None, :] * signs / safe)
    return offdiag - jnp.diag(jnp.sum(offdiag, axis=1))


small = pl.CostEstimate(flops=1024, bytes_accessed=1024, transcendentals=0)
heavy = pl.CostEstimate(flops=100000000000, bytes_accessed=1024, transcendentals=0)


def params():
    return pltpu.CompilerParams(vmem_limit_bytes=vmem_bytes)


def x_terms(u, c_xx, c_xy, sums):
    term_xx = 2.0 * sums[3] * c_xx - u * sums[0]
    term_xy = sums[3] * c_xy + sums[4] * c_xx - u * sums[1]
    term_yy = 2.0 * sums[4] * c_xy - u * sums[2]
    return term_xx, term_xy, term_yy


def from_after(planes, i, coeffs):
    return sum(coeffs[k - 1] * planes[i + k - width] for k in range(width - i, width + 1))


def from_before(planes, i, coeffs):
    return -sum(coeffs[k - 1] * planes[width + i - k] for k in range(i + 1, width + 1))


def inside(planes, i, coeffs):
    total = None
    for k in range(1, width):
        for at, sign in ((i + k, 1.0), (i - k, -1.0)):
            if 0 <= at < width:
                term = (sign * coeffs[k - 1]) * planes[at]
                total = term if total is None else total + term
    return total


def local_kernel(coeffs, lanes, step_ref, comp_ref, vel_ref, out_ref):
    step = step_ref[:, 0:1]
    for i in range(width):
        comp = [comp_ref[f, i] for f in range(3)]
        along_z = []
        for f in range(3):
            total = None
            for k in range(1, width + 1):
                ahead = pltpu.roll(comp[f], lanes - k, 1)
                behind = pltpu.roll(comp[f], k, 1)
                term = coeffs[k - 1] * (ahead - behind)
                total = term if total is None else total + term
            along_z.append(total)
        sums = [inside([comp_ref[f, j] for j in range(width)], i, coeffs) for f in range(3)]
        sums += [inside([vel_ref[f, j] for j in range(width)], i, coeffs) for f in range(2)]
        terms = x_terms(vel_ref[0, i], comp[0], comp[1], sums)
        peterlin = (extensibility - 2.0) / (extensibility - comp[0] - comp[2])
        rest = (1.0, 0.0, 1.0)
        w = vel_ref[2, i]
        for f in range(3):
            relax = relax_rate * (peterlin * comp[f] - rest[f])
            out_ref[f, i] = comp[f] + step * (terms[f] - w * along_z[f] - relax)


def pack_kernel(boxes, place_ref, comp_ref, vel_ref, *refs):
    outs, held, sems = refs[: len(boxes)], refs[len(boxes) : -1], refs[-1]
    loads, stores = [], []
    for j, (plane, n_planes, row, row_unit, n_rows, lane_unit, n_lanes) in enumerate(boxes):
        rows = pl.ds(pl.multiple_of(place_ref[j] * row_unit + row, row_block), n_rows)
        lanes = pl.ds(pl.multiple_of(place_ref[j] * lane_unit, 128), n_lanes)
        for source, first, fields in ((comp_ref, 0, 3), (vel_ref, 3, 2)):
            for f in range(fields):
                for p in range(n_planes):
                    k, to = len(loads), (first + f, p)
                    loads.append(pltpu.make_async_copy(source.at[f, plane + p, rows, lanes], held[j].at[to], sems.at[0, k]))
                    stores.append(pltpu.make_async_copy(held[j].at[to], outs[j].at[to], sems.at[1, k]))
    for load in loads:
        load.start()
    for load, store in zip(loads, stores):
        load.wait()
        store.start()
    for store in stores:
        store.wait()


def pack(places, boxes, comp, vel):
    here = pl.BlockSpec(memory_space=pltpu.HBM)
    shapes = [(5, planes, rows, lanes) for _, planes, _, _, rows, _, lanes in boxes]
    return pl.pallas_call(
        functools.partial(pack_kernel, boxes),
        in_specs=[pl.BlockSpec(memory_space=pltpu.SMEM), here, here],
        out_specs=[here] * len(boxes),
        out_shape=[jax.ShapeDtypeStruct(shape, jnp.float32) for shape in shapes],
        scratch_shapes=[pltpu.VMEM(shape, jnp.float32) for shape in shapes]
        + [pltpu.SemaphoreType.DMA((2, sum(5 * shape[1] for shape in shapes)))],
        compiler_params=params(),
        cost_estimate=small,
        name="pack",
    )(places, comp, vel)


def wall_kernel(groups, rows, *refs):
    comp_ref, vel_ref = refs[1:3]
    received = refs[3 : 2 + groups]
    matrix_ref, acc_ref = refs[2 + groups : 4 + groups]
    out_ref = refs[4 + groups]
    back = refs[5 + groups :]
    matrix = matrix_ref[...]
    fields, slopes = [], []
    for f in range(5):
        own = comp_ref[f, 0] if f < 3 else vel_ref[f - 3, 0]
        column = jnp.concatenate([own] + [r[f, 0] for r in received], axis=0)
        high = column.astype(jnp.bfloat16)
        low = (column - high.astype(jnp.float32)).astype(jnp.bfloat16)
        stacked = jnp.concatenate([high, low, high], axis=0)
        slopes.append(jnp.dot(matrix, stacked, preferred_element_type=jnp.float32))
        fields.append(column)
    c_xy, c_yy, v = fields[1], fields[2], fields[4]
    terms = (
        2.0 * slopes[3] * c_xy - v * slopes[0],
        slopes[3] * c_yy + slopes[4] * c_xy - v * slopes[1],
        2.0 * slopes[4] * c_yy - v * slopes[2],
    )
    for f in range(3):
        out_ref[f, 0] = acc_ref[f, 0] + terms[f][0:rows]
        for g in range(1, groups):
            back[g - 1][f, 0] = terms[f][g * rows : (g + 1) * rows]


def wall_part(first, skip, planes, place, comp, vel, received, matrix, acc):
    groups = len(received) + 1
    rows, lanes = comp.shape[2:]
    columns = lanes // groups
    tile = min(columns, 256)
    tiles = columns // tile
    own = lambda p, i, s: (0, first + p, 0, s[0] * tiles + i)
    own_block = pl.BlockSpec((3, 1, rows, tile), own)
    held = lambda p, i, s: (0, skip + p, 0, i)
    sent = lambda p, i, s: (0, p, 0, i)
    grid_spec = pltpu.PrefetchScalarGridSpec(
        num_scalar_prefetch=1,
        grid=(planes, tiles),
        in_specs=[own_block, pl.BlockSpec((2, 1, rows, tile), own)]
        + [pl.BlockSpec((5, 1, rows, tile), held)] * (groups - 1)
        + [pl.BlockSpec(matrix.shape, lambda p, i, s: (0, 0)), own_block],
        out_specs=[own_block] + [pl.BlockSpec((3, 1, rows, tile), sent)] * (groups - 1),
    )
    count = rows * groups
    shapes = [jax.ShapeDtypeStruct(acc.shape, jnp.float32)]
    shapes += [jax.ShapeDtypeStruct((3, planes, rows, columns), jnp.float32)] * (groups - 1)
    out = pl.pallas_call(
        functools.partial(wall_kernel, groups, rows),
        grid_spec=grid_spec,
        out_shape=shapes,
        input_output_aliases={3 + groups: 0},
        compiler_params=params(),
        cost_estimate=heavy,
        name="wall_part",
    )(place, comp, vel, *received, matrix, acc)
    return out[0], out[1:]


def border_kernel(coeffs, returns, lanes, flag_ref, step_ref, comp_ref, vel_ref, *refs):
    received, acc_ref, out_ref, back_ref = (refs[:1], *refs[1:]) if returns else (refs[:2], *refs[2:], None)
    tile = min(lanes, 256)

    def run(after):
        step = step_ref[:, 0:1]
        for at in range(0, lanes, tile):
            here = slice(at, at + tile)
            own = [[(comp_ref[f, i, :, here] if f < 3 else vel_ref[f - 3, i, :, here]) for i in range(width)] for f in range(5)]
            fields = [(received[0], f) for f in range(5)] if returns else [(received[f // 3], f % 3) for f in range(5)]
            other = [[r[f, i, :, here] for i in range(width)] for r, f in fields]
            to_mine, to_theirs = (from_after, from_before) if after else (from_before, from_after)
            for i in range(width):
                mine = [to_mine(other[f], i, coeffs) for f in range(5)]
                terms = x_terms(own[3][i], own[0][i], own[1][i], mine)
                for f in range(3):
                    out_ref[f, i, :, here] = acc_ref[f, i, :, here] + step * terms[f]
                if returns:
                    theirs = [to_theirs(own[f], i, coeffs) for f in range(5)]
                    returned = x_terms(other[3][i], other[0][i], other[1][i], theirs)
                    for f in range(3):
                        back_ref[f, i, :, here] = step * returned[f]

    pl.when(flag_ref[0] == 1)(lambda: run(True))
    pl.when(flag_ref[0] == 0)(lambda: run(False))


def border_part(returns, skip, size, flags, coeffs, step, comp, vel, received, acc):
    planes, lanes = comp.shape[1], comp.shape[3]
    here = lambda r, s: (0, 0, s[1] + r, 0)
    block = pl.BlockSpec((3, planes, row_block, lanes), here)
    held = lambda r, s: (0, 0, skip // row_block + r, 0)
    sent = lambda r, s: (0, 0, r, 0)
    grid_spec = pltpu.PrefetchScalarGridSpec(
        num_scalar_prefetch=1,
        grid=(size // row_block,),
        in_specs=[
            pl.BlockSpec((row_block, 128), lambda r, s: (s[1] + r, 0)),
            block,
            pl.BlockSpec((2, planes, row_block, lanes), here),
            *(pl.BlockSpec((min(x.shape[0], 5 - at), planes, row_block, lanes), held) for at, x in zip((0, 3), received)),
            block,
        ],
        out_specs=[block] + [pl.BlockSpec((3, planes, row_block, lanes), sent)] * returns,
    )
    out = pl.pallas_call(
        functools.partial(border_kernel, coeffs, returns, lanes),
        grid_spec=grid_spec,
        out_shape=[jax.ShapeDtypeStruct(acc.shape, jnp.float32)]
        + [jax.ShapeDtypeStruct((3, planes, size, lanes), jnp.float32)] * returns,
        input_output_aliases={4 + len(received): 0},
        compiler_params=params(),
        cost_estimate=heavy if returns else small,
        name="border_part",
    )(flags, step, comp, vel, *received, acc)
    return out


def first_kernel(coeffs, lanes, flag_ref, step_ref, comp_ref, vel_ref, comp_near, vel_near, out_ref):
    local_kernel(coeffs, lanes, step_ref, comp_ref, vel_ref, out_ref)
    border_kernel(coeffs, False, lanes, flag_ref, step_ref, comp_ref, vel_ref, comp_near, vel_near, out_ref, out_ref)


def first_part(flags, coeffs, step, comp, vel, comp_near, vel_near):
    fields, planes, rows, lanes = comp.shape
    at = lambda r, s: (0, 0, r, 0)
    block = pl.BlockSpec((fields, planes, row_block, lanes), at)
    two = pl.BlockSpec((2, planes, row_block, lanes), at)
    grid_spec = pltpu.PrefetchScalarGridSpec(
        num_scalar_prefetch=1,
        grid=(rows // row_block,),
        in_specs=[pl.BlockSpec((row_block, 128), lambda r, s: (r, 0)), block, block, block, two],
        out_specs=block,
    )
    return pl.pallas_call(
        functools.partial(first_kernel, coeffs, lanes),
        grid_spec=grid_spec,
        out_shape=jax.ShapeDtypeStruct(comp.shape, jnp.float32),
        compiler_params=params(),
        cost_estimate=small,
        name="first_part",
    )(flags, step, comp, vel, comp_near, vel_near)


def add_kernel(first, row, row_unit, lane_unit, place_ref, part_ref, acc_ref, out_ref, parts, sums, sems):
    fields, planes, size, lanes = part_ref.shape
    rows = pl.ds(pl.multiple_of(place_ref[0] * row_unit + row, row_block), size)
    columns = pl.ds(pl.multiple_of(place_ref[0] * lane_unit, 128), lanes)
    pieces = [(f, p) for f in range(fields) for p in range(planes)]
    loads, stores = [], []
    for k, (f, p) in enumerate(pieces):
        loads.append(
            (
                pltpu.make_async_copy(part_ref.at[f, p], parts.at[f, p], sems.at[0, k]),
                pltpu.make_async_copy(acc_ref.at[f, first + p, rows, columns], sums.at[f, p], sems.at[1, k]),
            )
        )
        stores.append(pltpu.make_async_copy(parts.at[f, p], out_ref.at[f, first + p, rows, columns], sems.at[2, k]))
    for pair in loads:
        for load in pair:
            load.start()
    for (f, p), pair, store in zip(pieces, loads, stores):
        for load in pair:
            load.wait()
        parts[f, p] = parts[f, p] + sums[f, p]
        store.start()
    for store in stores:
        store.wait()


def add_part(first, row, row_unit, lane_unit, place, part, acc):
    here = pl.BlockSpec(memory_space=pltpu.HBM)
    return pl.pallas_call(
        functools.partial(add_kernel, first, row, row_unit, lane_unit),
        in_specs=[pl.BlockSpec(memory_space=pltpu.SMEM), pl.BlockSpec(memory_space=pl.ANY), here],
        out_specs=here,
        out_shape=jax.ShapeDtypeStruct(acc.shape, jnp.float32),
        input_output_aliases={2: 0},
        scratch_shapes=[pltpu.VMEM(part.shape, jnp.float32)] * 2
        + [pltpu.SemaphoreType.DMA((3, part.shape[0] * part.shape[1]))],
        compiler_params=pltpu.CompilerParams(vmem_limit_bytes=24 * 1024 * 1024),
        cost_estimate=small,
        name="add_part",
    )(place, part, acc)


def shares(total, unit):
    flat = [w for share in share_weights for w in share]
    ends = [unit * round(total // unit * sum(flat[:k]) / sum(flat)) for k in range(len(flat) + 1)]
    cuts, k = [], 0
    for share in share_weights:
        own = [(a, b - a) for a, b in zip(ends[k:], ends[k + 1 : k + 1 + len(share)]) if b > a]
        cuts.append((ends[k], ends[k + len(share)] - ends[k], own))
        k += len(share)
    return [cut for cut in cuts if cut[1]]


def shards(conformation, velocity):
    planes, rows, lanes = conformation.shape[1:]
    groups, slabs = lax.axis_size("yz"), lax.axis_size("gx")
    me, slab = lax.axis_index("yz"), lax.axis_index("gx")
    odd = (slab % 2).astype(jnp.int32)
    count = rows * groups
    columns = lanes // groups
    spacing = math.pi / (count - 1)
    coeffs = tuple(c / spacing for c in stencil_coeffs)
    half = rows // 2
    wall_cuts = shares(planes, 1)
    border_cuts = shares(half, row_block)
    near = [(i, i ^ 1) for i in range(slabs)]
    far = [(i, (i + 1 if i % 2 else i - 1) % slabs) for i in range(slabs)]

    def along_yz(x, by):
        return lax.ppermute(x, "yz", [(i, (i + by) % groups) for i in range(groups)])

    beside = [lax.ppermute(x, "gx", near) for x in (conformation, velocity)]
    walls, borders = [], []
    for k in range(len(share_weights)):
        places, boxes = [], []
        for plane, n_planes, _ in wall_cuts[k : k + 1]:
            places += [(me + g) % groups for g in range(1, groups)]
            boxes += [(plane, n_planes, 0, 0, rows, columns, columns)] * (groups - 1)
        for row, n_rows, _ in border_cuts[k : k + 1]:
            places.append(odd)
            boxes.append((0, planes, row, half, n_rows, 0, lanes))
        packed = [
            pack(place.astype(jnp.int32).reshape(1), [box], conformation, velocity)[0] for place, box in zip(places, boxes)
        ]
        if k < len(wall_cuts):
            walls.append([along_yz(packed[g - 1], g) for g in range(1, groups)][::-1])
        if k < len(border_cuts):
            borders.append(lax.ppermute(packed[-1], "gx", far))

    index = jnp.arange(count, dtype=jnp.int32)
    points = index % rows * groups + (index // rows + me) % groups
    theta = math.pi * points.astype(jnp.float32) / (count - 1)
    step_size = courant * spacing * (jnp.sin(theta) + spacing)
    cheb = step_size[:, None] * cheb_matrix(count, points)
    high = lax.reduce_precision(cheb, 8, 7)
    low = lax.reduce_precision(cheb - high, 8, 7)
    matrix = jnp.concatenate([high, high, low], axis=1).astype(jnp.bfloat16)
    step = jnp.broadcast_to(step_size[:rows, None], (rows, 128))

    acc = first_part((1 - odd).reshape(1), coeffs, step, conformation, velocity, *beside)
    place = me.astype(jnp.int32).reshape(1)
    returned = []
    for k in range(len(share_weights)):
        wall_own = wall_cuts[k][2] if k < len(wall_cuts) else []
        border_own = border_cuts[k][2] if k < len(border_cuts) else []
        for j in range(max(len(wall_own), len(border_own))):
            if j < len(wall_own):
                at, size = wall_own[j]
                acc, back = wall_part(
                    at, at - wall_cuts[k][0], size, place, conformation, velocity, walls[k], matrix, acc
                )
                for g, b in enumerate(back, 1):
                    source = ((me - g) % groups).astype(jnp.int32).reshape(1)
                    returned.append((at, 0, 0, columns, source, along_yz(b, g)))
            if j < len(border_own):
                at, size = border_own[j]
                far_flags = jnp.stack([odd, ((1 - odd) * half + at) // row_block])
                acc, back = border_part(
                    True, at - border_cuts[k][0], size, far_flags, coeffs, step, conformation, velocity, [borders[k]], acc
                )
                returned.append((0, at, half, 0, odd.reshape(1), lax.ppermute(back, "gx", far)))
    for first, row, row_unit, lane_unit, source, part in returned:
        acc = add_part(first, row, row_unit, lane_unit, source, part, acc)
    return acc


def solution(mesh):
    in_specs = (P(None, "gx", "yz", None), P(None, "gx", "yz", None))
    out_specs = P(None, "gx", "yz", None)
    return jax.shard_map(shards, mesh=mesh, in_specs=in_specs, out_specs=out_specs, check_vma=False)
```

```python
import functools
import math

import jax
import jax.numpy as jnp
from jax import lax
from jax.experimental import pallas as pl
from jax.experimental.pallas import tpu as pltpu
from jax.sharding import PartitionSpec as P

stencil_coeffs = (0.8, -0.2, 4.0 / 105.0, -1.0 / 280.0)
width = 4
extensibility = 10.0
relax_rate = 1.0 / 0.04
courant = 0.5
row_block = 8
share_weights = ((3,), (7, 2))
vmem_bytes = 56 * 1024 * 1024


def cheb_matrix(count, points):
    last = count - 1
    half_step = math.pi / (2.0 * last)
    weights = jnp.where((points == 0) | (points == last), 2.0, 1.0).astype(jnp.float32)
    same = points[:, None] == points[None, :]
    sums = (points[:, None] + points[None, :]).astype(jnp.float32) * half_step
    diffs = (points[:, None] - points[None, :]).astype(jnp.float32) * half_step
    signs = (1 - 2 * ((points[:, None] + points[None, :]) % 2)).astype(jnp.float32)
    apart = -2.0 * jnp.sin(sums) * jnp.sin(diffs)
    safe = jnp.where(same, 1.0, apart)
    offdiag = jnp.where(same, 0.0, weights[:, None] / weights[None, :] * signs / safe)
    return offdiag - jnp.diag(jnp.sum(offdiag, axis=1))


small = pl.CostEstimate(flops=1024, bytes_accessed=1024, transcendentals=0)
heavy = pl.CostEstimate(flops=100000000000, bytes_accessed=1024, transcendentals=0)


def params():
    return pltpu.CompilerParams(vmem_limit_bytes=vmem_bytes)


def x_terms(u, c_xx, c_xy, sums):
    term_xx = 2.0 * sums[3] * c_xx - u * sums[0]
    term_xy = sums[3] * c_xy + sums[4] * c_xx - u * sums[1]
    term_yy = 2.0 * sums[4] * c_xy - u * sums[2]
    return term_xx, term_xy, term_yy


def from_after(planes, i, coeffs):
    return sum(coeffs[k - 1] * planes[i + k - width] for k in range(width - i, width + 1))


def from_before(planes, i, coeffs):
    return -sum(coeffs[k - 1] * planes[width + i - k] for k in range(i + 1, width + 1))


def inside(planes, i, coeffs):
    total = None
    for k in range(1, width):
        for at, sign in ((i + k, 1.0), (i - k, -1.0)):
            if 0 <= at < width:
                term = (sign * coeffs[k - 1]) * planes[at]
                total = term if total is None else total + term
    return total


def local_kernel(coeffs, lanes, step_ref, comp_ref, vel_ref, out_ref):
    step = step_ref[:, 0:1]
    for i in range(width):
        comp = [comp_ref[f, i] for f in range(3)]
        along_z = []
        for f in range(3):
            total = None
            for k in range(1, width + 1):
                ahead = pltpu.roll(comp[f], lanes - k, 1)
                behind = pltpu.roll(comp[f], k, 1)
                term = coeffs[k - 1] * (ahead - behind)
                total = term if total is None else total + term
            along_z.append(total)
        sums = [inside([comp_ref[f, j] for j in range(width)], i, coeffs) for f in range(3)]
        sums += [inside([vel_ref[f, j] for j in range(width)], i, coeffs) for f in range(2)]
        terms = x_terms(vel_ref[0, i], comp[0], comp[1], sums)
        peterlin = (extensibility - 2.0) / (extensibility - comp[0] - comp[2])
        rest = (1.0, 0.0, 1.0)
        w = vel_ref[2, i]
        for f in range(3):
            relax = relax_rate * (peterlin * comp[f] - rest[f])
            out_ref[f, i] = comp[f] + step * (terms[f] - w * along_z[f] - relax)


def pack_kernel(boxes, direct, place_ref, comp_ref, vel_ref, *refs):
    outs, held, sems = refs[: len(boxes)], refs[: len(boxes)] if direct else refs[len(boxes) : -1], refs[-1]
    loads, stores = [], []
    for j, (plane, n_planes, row, row_unit, n_rows, lane_unit, n_lanes) in enumerate(boxes):
        rows = pl.ds(pl.multiple_of(place_ref[j] * row_unit + row, row_block), n_rows)
        lanes = pl.ds(pl.multiple_of(place_ref[j] * lane_unit, 128), n_lanes)
        for source, first, fields in ((comp_ref, 0, 3), (vel_ref, 3, 2)):
            for f in range(fields):
                for p in range(n_planes):
                    k, to = len(loads), (first + f, p)
                    loads.append(pltpu.make_async_copy(source.at[f, plane + p, rows, lanes], held[j].at[to], sems.at[0, k]))
                    if not direct:
                        stores.append(pltpu.make_async_copy(held[j].at[to], outs[j].at[to], sems.at[1, k]))
    for load in loads:
        load.start()
    for k, load in enumerate(loads):
        load.wait()
        if not direct:
            stores[k].start()
    for store in stores:
        store.wait()


def pack(places, boxes, direct, comp, vel):
    here = pl.BlockSpec(memory_space=pltpu.HBM)
    shapes = [(5, planes, rows, lanes) for _, planes, _, _, rows, _, lanes in boxes]
    return pl.pallas_call(
        functools.partial(pack_kernel, boxes, direct),
        in_specs=[pl.BlockSpec(memory_space=pltpu.SMEM), here, here],
        out_specs=[pl.BlockSpec(memory_space=pltpu.VMEM) if direct else here] * len(boxes),
        out_shape=[pltpu.VMEM(shape, jnp.float32) if direct else jax.ShapeDtypeStruct(shape, jnp.float32) for shape in shapes],
        scratch_shapes=[pltpu.VMEM(shape, jnp.float32) for shape in shapes if not direct]
        + [pltpu.SemaphoreType.DMA((2, sum(5 * shape[1] for shape in shapes)))],
        compiler_params=params(),
        cost_estimate=small,
        name="pack",
    )(places, comp, vel)


def wall_kernel(groups, rows, *refs):
    comp_ref, vel_ref = refs[1:3]
    received = refs[3 : 2 + groups]
    matrix_ref, acc_ref = refs[2 + groups : 4 + groups]
    out_ref = refs[4 + groups]
    back = refs[5 + groups :]
    matrix = matrix_ref[...]
    fields, slopes = [], []
    for f in range(5):
        own = comp_ref[f, 0] if f < 3 else vel_ref[f - 3, 0]
        column = jnp.concatenate([own] + [r[f, 0] for r in received], axis=0)
        high = column.astype(jnp.bfloat16)
        low = (column - high.astype(jnp.float32)).astype(jnp.bfloat16)
        stacked = jnp.concatenate([high, low, high], axis=0)
        slopes.append(jnp.dot(matrix, stacked, preferred_element_type=jnp.float32))
        fields.append(column)
    c_xy, c_yy, v = fields[1], fields[2], fields[4]
    terms = (
        2.0 * slopes[3] * c_xy - v * slopes[0],
        slopes[3] * c_yy + slopes[4] * c_xy - v * slopes[1],
        2.0 * slopes[4] * c_yy - v * slopes[2],
    )
    for f in range(3):
        out_ref[f, 0] = acc_ref[f, 0] + terms[f][0:rows]
        for g in range(1, groups):
            back[g - 1][f, 0] = terms[f][g * rows : (g + 1) * rows]


def wall_part(first, skip, planes, place, comp, vel, received, matrix, acc):
    groups = len(received) + 1
    rows, lanes = comp.shape[2:]
    columns = lanes // groups
    tile = min(columns, 256)
    tiles = columns // tile
    own = lambda p, i, s: (0, first + p, 0, s[0] * tiles + i)
    own_block = pl.BlockSpec((3, 1, rows, tile), own)
    held = lambda p, i, s: (0, skip + p, 0, i)
    sent = lambda p, i, s: (0, p, 0, i)
    grid_spec = pltpu.PrefetchScalarGridSpec(
        num_scalar_prefetch=1,
        grid=(planes, tiles),
        in_specs=[own_block, pl.BlockSpec((2, 1, rows, tile), own)]
        + [pl.BlockSpec((5, 1, rows, tile), held)] * (groups - 1)
        + [pl.BlockSpec(matrix.shape, lambda p, i, s: (0, 0)), own_block],
        out_specs=[own_block] + [pl.BlockSpec((3, 1, rows, tile), sent)] * (groups - 1),
    )
    count = rows * groups
    shapes = [jax.ShapeDtypeStruct(acc.shape, jnp.float32)]
    shapes += [jax.ShapeDtypeStruct((3, planes, rows, columns), jnp.float32)] * (groups - 1)
    out = pl.pallas_call(
        functools.partial(wall_kernel, groups, rows),
        grid_spec=grid_spec,
        out_shape=shapes,
        input_output_aliases={3 + groups: 0},
        compiler_params=params(),
        cost_estimate=heavy,
        name="wall_part",
    )(place, comp, vel, *received, matrix, acc)
    return out[0], out[1:]


def border_kernel(coeffs, returns, lanes, flag_ref, step_ref, comp_ref, vel_ref, *refs):
    received, acc_ref, out_ref, back_ref = (refs[:1], *refs[1:]) if returns else (refs[:2], *refs[2:], None)
    tile = min(lanes, 256)

    def run(after):
        step = step_ref[:, 0:1]
        for at in range(0, lanes, tile):
            here = slice(at, at + tile)
            own = [[(comp_ref[f, i, :, here] if f < 3 else vel_ref[f - 3, i, :, here]) for i in range(width)] for f in range(5)]
            fields = [(received[0], f) for f in range(5)] if returns else [(received[f // 3], f % 3) for f in range(5)]
            other = [[r[f, i, :, here] for i in range(width)] for r, f in fields]
            to_mine, to_theirs = (from_after, from_before) if after else (from_before, from_after)
            for i in range(width):
                mine = [to_mine(other[f], i, coeffs) for f in range(5)]
                terms = x_terms(own[3][i], own[0][i], own[1][i], mine)
                for f in range(3):
                    out_ref[f, i, :, here] = acc_ref[f, i, :, here] + step * terms[f]
                if returns:
                    theirs = [to_theirs(own[f], i, coeffs) for f in range(5)]
                    returned = x_terms(other[3][i], other[0][i], other[1][i], theirs)
                    for f in range(3):
                        back_ref[f, i, :, here] = step * returned[f]

    pl.when(flag_ref[0] == 1)(lambda: run(True))
    pl.when(flag_ref[0] == 0)(lambda: run(False))


def border_part(returns, skip, size, flags, coeffs, step, comp, vel, received, acc):
    planes, lanes = comp.shape[1], comp.shape[3]
    here = lambda r, s: (0, 0, s[1] + r, 0)
    block = pl.BlockSpec((3, planes, row_block, lanes), here)
    held = lambda r, s: (0, 0, skip // row_block + r, 0)
    sent = lambda r, s: (0, 0, r, 0)
    grid_spec = pltpu.PrefetchScalarGridSpec(
        num_scalar_prefetch=1,
        grid=(size // row_block,),
        in_specs=[
            pl.BlockSpec((row_block, 128), lambda r, s: (s[1] + r, 0)),
            block,
            pl.BlockSpec((2, planes, row_block, lanes), here),
            *(pl.BlockSpec((min(x.shape[0], 5 - at), planes, row_block, lanes), held) for at, x in zip((0, 3), received)),
            block,
        ],
        out_specs=[block] + [pl.BlockSpec((3, planes, row_block, lanes), sent)] * returns,
    )
    out = pl.pallas_call(
        functools.partial(border_kernel, coeffs, returns, lanes),
        grid_spec=grid_spec,
        out_shape=[jax.ShapeDtypeStruct(acc.shape, jnp.float32)]
        + [jax.ShapeDtypeStruct((3, planes, size, lanes), jnp.float32)] * returns,
        input_output_aliases={4 + len(received): 0},
        compiler_params=params(),
        cost_estimate=heavy if returns else small,
        name="border_part",
    )(flags, step, comp, vel, *received, acc)
    return out


def first_kernel(coeffs, lanes, flag_ref, step_ref, comp_ref, vel_ref, comp_near, vel_near, out_ref):
    local_kernel(coeffs, lanes, step_ref, comp_ref, vel_ref, out_ref)
    border_kernel(coeffs, False, lanes, flag_ref, step_ref, comp_ref, vel_ref, comp_near, vel_near, out_ref, out_ref)


def first_part(flags, coeffs, step, comp, vel, comp_near, vel_near):
    fields, planes, rows, lanes = comp.shape
    at = lambda r, s: (0, 0, r, 0)
    block = pl.BlockSpec((fields, planes, row_block, lanes), at)
    two = pl.BlockSpec((2, planes, row_block, lanes), at)
    grid_spec = pltpu.PrefetchScalarGridSpec(
        num_scalar_prefetch=1,
        grid=(rows // row_block,),
        in_specs=[pl.BlockSpec((row_block, 128), lambda r, s: (r, 0)), block, block, block, two],
        out_specs=block,
    )
    return pl.pallas_call(
        functools.partial(first_kernel, coeffs, lanes),
        grid_spec=grid_spec,
        out_shape=jax.ShapeDtypeStruct(comp.shape, jnp.float32),
        compiler_params=params(),
        cost_estimate=small,
        name="first_part",
    )(flags, step, comp, vel, comp_near, vel_near)


def add_kernel(first, row, row_unit, lane_unit, place_ref, part_ref, acc_ref, out_ref, parts, sums, sems):
    fields, planes, size, lanes = part_ref.shape
    rows = pl.ds(pl.multiple_of(place_ref[0] * row_unit + row, row_block), size)
    columns = pl.ds(pl.multiple_of(place_ref[0] * lane_unit, 128), lanes)
    pieces = [(f, p) for f in range(fields) for p in range(planes)]
    loads, stores = [], []
    for k, (f, p) in enumerate(pieces):
        loads.append(
            (
                pltpu.make_async_copy(part_ref.at[f, p], parts.at[f, p], sems.at[0, k]),
                pltpu.make_async_copy(acc_ref.at[f, first + p, rows, columns], sums.at[f, p], sems.at[1, k]),
            )
        )
        stores.append(pltpu.make_async_copy(parts.at[f, p], out_ref.at[f, first + p, rows, columns], sems.at[2, k]))
    for pair in loads:
        for load in pair:
            load.start()
    for (f, p), pair, store in zip(pieces, loads, stores):
        for load in pair:
            load.wait()
        parts[f, p] = parts[f, p] + sums[f, p]
        store.start()
    for store in stores:
        store.wait()


def add_part(first, row, row_unit, lane_unit, place, part, acc):
    here = pl.BlockSpec(memory_space=pltpu.HBM)
    return pl.pallas_call(
        functools.partial(add_kernel, first, row, row_unit, lane_unit),
        in_specs=[pl.BlockSpec(memory_space=pltpu.SMEM), pl.BlockSpec(memory_space=pl.ANY), here],
        out_specs=here,
        out_shape=jax.ShapeDtypeStruct(acc.shape, jnp.float32),
        input_output_aliases={2: 0},
        scratch_shapes=[pltpu.VMEM(part.shape, jnp.float32)] * 2
        + [pltpu.SemaphoreType.DMA((3, part.shape[0] * part.shape[1]))],
        compiler_params=pltpu.CompilerParams(vmem_limit_bytes=24 * 1024 * 1024),
        cost_estimate=small,
        name="add_part",
    )(place, part, acc)


def shares(total, unit):
    flat = [w for share in share_weights for w in share]
    ends = [unit * round(total // unit * sum(flat[:k]) / sum(flat)) for k in range(len(flat) + 1)]
    cuts, k = [], 0
    for share in share_weights:
        own = [(a, b - a) for a, b in zip(ends[k:], ends[k + 1 : k + 1 + len(share)]) if b > a]
        cuts.append((ends[k], ends[k + len(share)] - ends[k], own))
        k += len(share)
    return [cut for cut in cuts if cut[1]]


def shards(conformation, velocity):
    planes, rows, lanes = conformation.shape[1:]
    groups, slabs = lax.axis_size("yz"), lax.axis_size("gx")
    me, slab = lax.axis_index("yz"), lax.axis_index("gx")
    odd = (slab % 2).astype(jnp.int32)
    count = rows * groups
    columns = lanes // groups
    spacing = math.pi / (count - 1)
    coeffs = tuple(c / spacing for c in stencil_coeffs)
    half = rows // 2
    wall_cuts = shares(planes, 1)
    border_cuts = shares(half, row_block)
    near = [(i, i ^ 1) for i in range(slabs)]
    far = [(i, (i + 1 if i % 2 else i - 1) % slabs) for i in range(slabs)]

    def along_yz(x, by):
        return lax.ppermute(x, "yz", [(i, (i + by) % groups) for i in range(groups)])

    beside = [lax.ppermute(x, "gx", near) for x in (conformation, velocity)]
    walls, borders = [], []
    for k in range(len(share_weights)):
        places, boxes = [], []
        for plane, n_planes, _ in wall_cuts[k : k + 1]:
            places += [(me + g) % groups for g in range(1, groups)]
            boxes += [(plane, n_planes, 0, 0, rows, columns, columns)] * (groups - 1)
        for row, n_rows, _ in border_cuts[k : k + 1]:
            places.append(odd)
            boxes.append((0, planes, row, half, n_rows, 0, lanes))
        packed = [
            pack(place.astype(jnp.int32).reshape(1), [box], k == 0 and box[-2] > 0, conformation, velocity)[0] for place, box in zip(places, boxes)
        ]
        if k < len(wall_cuts):
            walls.append([along_yz(packed[g - 1], g) for g in range(1, groups)][::-1])
        if k < len(border_cuts):
            borders.append(lax.ppermute(packed[-1], "gx", far))

    index = jnp.arange(count, dtype=jnp.int32)
    points = index % rows * groups + (index // rows + me) % groups
    theta = math.pi * points.astype(jnp.float32) / (count - 1)
    step_size = courant * spacing * (jnp.sin(theta) + spacing)
    cheb = step_size[:, None] * cheb_matrix(count, points)
    high = lax.reduce_precision(cheb, 8, 7)
    low = lax.reduce_precision(cheb - high, 8, 7)
    matrix = jnp.concatenate([high, high, low], axis=1).astype(jnp.bfloat16)
    step = jnp.broadcast_to(step_size[:rows, None], (rows, 128))

    acc = first_part((1 - odd).reshape(1), coeffs, step, conformation, velocity, *beside)
    place = me.astype(jnp.int32).reshape(1)
    returned = []
    for k in range(len(share_weights)):
        wall_own = wall_cuts[k][2] if k < len(wall_cuts) else []
        border_own = border_cuts[k][2] if k < len(border_cuts) else []
        for j in range(max(len(wall_own), len(border_own))):
            if j < len(wall_own):
                at, size = wall_own[j]
                acc, back = wall_part(
                    at, at - wall_cuts[k][0], size, place, conformation, velocity, walls[k], matrix, acc
                )
                for g, b in enumerate(back, 1):
                    source = ((me - g) % groups).astype(jnp.int32).reshape(1)
                    returned.append((at, 0, 0, columns, source, along_yz(b, g)))
            if j < len(border_own):
                at, size = border_own[j]
                far_flags = jnp.stack([odd, ((1 - odd) * half + at) // row_block])
                acc, back = border_part(
                    True, at - border_cuts[k][0], size, far_flags, coeffs, step, conformation, velocity, [borders[k]], acc
                )
                returned.append((0, at, half, 0, odd.reshape(1), lax.ppermute(back, "gx", far)))
    for first, row, row_unit, lane_unit, source, part in returned:
        acc = add_part(first, row, row_unit, lane_unit, source, part, acc)
    return acc


def solution(mesh):
    in_specs = (P(None, "gx", "yz", None), P(None, "gx", "yz", None))
    out_specs = P(None, "gx", "yz", None)
    return jax.shard_map(shards, mesh=mesh, in_specs=in_specs, out_specs=out_specs, check_vma=False)
```

```python
import functools
import math

import jax
import jax.numpy as jnp
from jax import lax
from jax.experimental import pallas as pl
from jax.experimental.pallas import tpu as pltpu
from jax.sharding import PartitionSpec as P

stencil_coeffs = (0.8, -0.2, 4.0 / 105.0, -1.0 / 280.0)
width = 4
extensibility = 10.0
relax_rate = 1.0 / 0.04
courant = 0.5
row_block = 8
share_weights = ((3,), (7, 2))
vmem_bytes = 56 * 1024 * 1024


def cheb_matrix(count, points):
    last = count - 1
    half_step = math.pi / (2.0 * last)
    weights = jnp.where((points == 0) | (points == last), 2.0, 1.0).astype(jnp.float32)
    same = points[:, None] == points[None, :]
    sums = (points[:, None] + points[None, :]).astype(jnp.float32) * half_step
    diffs = (points[:, None] - points[None, :]).astype(jnp.float32) * half_step
    signs = (1 - 2 * ((points[:, None] + points[None, :]) % 2)).astype(jnp.float32)
    apart = -2.0 * jnp.sin(sums) * jnp.sin(diffs)
    safe = jnp.where(same, 1.0, apart)
    offdiag = jnp.where(same, 0.0, weights[:, None] / weights[None, :] * signs / safe)
    return offdiag - jnp.diag(jnp.sum(offdiag, axis=1))


small = pl.CostEstimate(flops=1024, bytes_accessed=1024, transcendentals=0)
heavy = pl.CostEstimate(flops=100000000000, bytes_accessed=1024, transcendentals=0)


def params():
    return pltpu.CompilerParams(vmem_limit_bytes=vmem_bytes)


def x_terms(u, c_xx, c_xy, sums):
    term_xx = 2.0 * sums[3] * c_xx - u * sums[0]
    term_xy = sums[3] * c_xy + sums[4] * c_xx - u * sums[1]
    term_yy = 2.0 * sums[4] * c_xy - u * sums[2]
    return term_xx, term_xy, term_yy


def from_after(planes, i, coeffs):
    return sum(coeffs[k - 1] * planes[i + k - width] for k in range(width - i, width + 1))


def from_before(planes, i, coeffs):
    return -sum(coeffs[k - 1] * planes[width + i - k] for k in range(i + 1, width + 1))


def inside(planes, i, coeffs):
    total = None
    for k in range(1, width):
        for at, sign in ((i + k, 1.0), (i - k, -1.0)):
            if 0 <= at < width:
                term = (sign * coeffs[k - 1]) * planes[at]
                total = term if total is None else total + term
    return total


def local_kernel(coeffs, lanes, step_ref, comp_ref, vel_ref, out_ref):
    step = step_ref[:, 0:1]
    for i in range(width):
        comp = [comp_ref[f, i] for f in range(3)]
        along_z = []
        for f in range(3):
            total = None
            for k in range(1, width + 1):
                ahead = pltpu.roll(comp[f], lanes - k, 1)
                behind = pltpu.roll(comp[f], k, 1)
                term = coeffs[k - 1] * (ahead - behind)
                total = term if total is None else total + term
            along_z.append(total)
        sums = [inside([comp_ref[f, j] for j in range(width)], i, coeffs) for f in range(3)]
        sums += [inside([vel_ref[f, j] for j in range(width)], i, coeffs) for f in range(2)]
        terms = x_terms(vel_ref[0, i], comp[0], comp[1], sums)
        peterlin = (extensibility - 2.0) / (extensibility - comp[0] - comp[2])
        rest = (1.0, 0.0, 1.0)
        w = vel_ref[2, i]
        for f in range(3):
            relax = relax_rate * (peterlin * comp[f] - rest[f])
            out_ref[f, i] = comp[f] + step * (terms[f] - w * along_z[f] - relax)


def pack_kernel(boxes, direct, place_ref, comp_ref, vel_ref, *refs):
    outs, held, sems = refs[: len(boxes)], refs[: len(boxes)] if direct else refs[len(boxes) : -1], refs[-1]
    loads, stores = [], []
    for j, (plane, n_planes, row, row_unit, n_rows, lane_unit, n_lanes) in enumerate(boxes):
        rows = pl.ds(pl.multiple_of(place_ref[j] * row_unit + row, row_block), n_rows)
        lanes = pl.ds(pl.multiple_of(place_ref[j] * lane_unit, 128), n_lanes)
        for source, first, fields in ((comp_ref, 0, 3), (vel_ref, 3, 2)):
            for f in range(fields):
                k, to = len(loads), first + f
                planes = pl.ds(plane, n_planes)
                loads.append(pltpu.make_async_copy(source.at[f, planes, rows, lanes], held[j].at[to], sems.at[0, k]))
                if not direct:
                    stores.append(pltpu.make_async_copy(held[j].at[to], outs[j].at[to], sems.at[1, k]))
    for load in loads:
        load.start()
    for k, load in enumerate(loads):
        load.wait()
        if not direct:
            stores[k].start()
    for store in stores:
        store.wait()


def pack(places, boxes, direct, comp, vel):
    here = pl.BlockSpec(memory_space=pltpu.HBM)
    shapes = [(5, planes, rows, lanes) for _, planes, _, _, rows, _, lanes in boxes]
    return pl.pallas_call(
        functools.partial(pack_kernel, boxes, direct),
        in_specs=[pl.BlockSpec(memory_space=pltpu.SMEM), here, here],
        out_specs=[pl.BlockSpec(memory_space=pltpu.VMEM) if direct else here] * len(boxes),
        out_shape=[pltpu.VMEM(shape, jnp.float32) if direct else jax.ShapeDtypeStruct(shape, jnp.float32) for shape in shapes],
        scratch_shapes=[pltpu.VMEM(shape, jnp.float32) for shape in shapes if not direct]
        + [pltpu.SemaphoreType.DMA((2, 5 * len(boxes)))],
        compiler_params=params(),
        cost_estimate=small,
        name="pack",
    )(places, comp, vel)


def wall_kernel(groups, rows, *refs):
    comp_ref, vel_ref = refs[1:3]
    received = refs[3 : 2 + groups]
    matrix_ref, acc_ref = refs[2 + groups : 4 + groups]
    out_ref = refs[4 + groups]
    back = refs[5 + groups :]
    matrix = matrix_ref[...]
    fields, slopes = [], []
    for f in range(5):
        own = comp_ref[f, 0] if f < 3 else vel_ref[f - 3, 0]
        column = jnp.concatenate([own] + [r[f, 0] for r in received], axis=0)
        high = column.astype(jnp.bfloat16)
        low = (column - high.astype(jnp.float32)).astype(jnp.bfloat16)
        stacked = jnp.concatenate([high, low, high], axis=0)
        slopes.append(jnp.dot(matrix, stacked, preferred_element_type=jnp.float32))
        fields.append(column)
    c_xy, c_yy, v = fields[1], fields[2], fields[4]
    terms = (
        2.0 * slopes[3] * c_xy - v * slopes[0],
        slopes[3] * c_yy + slopes[4] * c_xy - v * slopes[1],
        2.0 * slopes[4] * c_yy - v * slopes[2],
    )
    for f in range(3):
        out_ref[f, 0] = acc_ref[f, 0] + terms[f][0:rows]
        for g in range(1, groups):
            back[g - 1][f, 0] = terms[f][g * rows : (g + 1) * rows]


def wall_part(first, skip, planes, place, comp, vel, received, matrix, acc):
    groups = len(received) + 1
    rows, lanes = comp.shape[2:]
    columns = lanes // groups
    tile = min(columns, 256)
    tiles = columns // tile
    own = lambda p, i, s: (0, first + p, 0, s[0] * tiles + i)
    own_block = pl.BlockSpec((3, 1, rows, tile), own)
    held = lambda p, i, s: (0, skip + p, 0, i)
    sent = lambda p, i, s: (0, p, 0, i)
    grid_spec = pltpu.PrefetchScalarGridSpec(
        num_scalar_prefetch=1,
        grid=(planes, tiles),
        in_specs=[own_block, pl.BlockSpec((2, 1, rows, tile), own)]
        + [pl.BlockSpec((5, 1, rows, tile), held)] * (groups - 1)
        + [pl.BlockSpec(matrix.shape, lambda p, i, s: (0, 0)), own_block],
        out_specs=[own_block] + [pl.BlockSpec((3, 1, rows, tile), sent)] * (groups - 1),
    )
    count = rows * groups
    shapes = [jax.ShapeDtypeStruct(acc.shape, jnp.float32)]
    shapes += [jax.ShapeDtypeStruct((3, planes, rows, columns), jnp.float32)] * (groups - 1)
    out = pl.pallas_call(
        functools.partial(wall_kernel, groups, rows),
        grid_spec=grid_spec,
        out_shape=shapes,
        input_output_aliases={3 + groups: 0},
        compiler_params=params(),
        cost_estimate=heavy,
        name="wall_part",
    )(place, comp, vel, *received, matrix, acc)
    return out[0], out[1:]


def border_kernel(coeffs, returns, lanes, flag_ref, step_ref, comp_ref, vel_ref, *refs):
    received, acc_ref, out_ref, back_ref = (refs[:1], *refs[1:]) if returns else (refs[:2], *refs[2:], None)
    tile = min(lanes, 256)

    def run(after):
        step = step_ref[:, 0:1]
        for at in range(0, lanes, tile):
            here = slice(at, at + tile)
            own = [[(comp_ref[f, i, :, here] if f < 3 else vel_ref[f - 3, i, :, here]) for i in range(width)] for f in range(5)]
            fields = [(received[0], f) for f in range(5)] if returns else [(received[f // 3], f % 3) for f in range(5)]
            other = [[r[f, i, :, here] for i in range(width)] for r, f in fields]
            to_mine, to_theirs = (from_after, from_before) if after else (from_before, from_after)
            for i in range(width):
                mine = [to_mine(other[f], i, coeffs) for f in range(5)]
                terms = x_terms(own[3][i], own[0][i], own[1][i], mine)
                for f in range(3):
                    out_ref[f, i, :, here] = acc_ref[f, i, :, here] + step * terms[f]
                if returns:
                    theirs = [to_theirs(own[f], i, coeffs) for f in range(5)]
                    returned = x_terms(other[3][i], other[0][i], other[1][i], theirs)
                    for f in range(3):
                        back_ref[f, i, :, here] = step * returned[f]

    pl.when(flag_ref[0] == 1)(lambda: run(True))
    pl.when(flag_ref[0] == 0)(lambda: run(False))


def border_part(returns, skip, size, flags, coeffs, step, comp, vel, received, acc):
    planes, lanes = comp.shape[1], comp.shape[3]
    here = lambda r, s: (0, 0, s[1] + r, 0)
    block = pl.BlockSpec((3, planes, row_block, lanes), here)
    held = lambda r, s: (0, 0, skip // row_block + r, 0)
    sent = lambda r, s: (0, 0, r, 0)
    grid_spec = pltpu.PrefetchScalarGridSpec(
        num_scalar_prefetch=1,
        grid=(size // row_block,),
        in_specs=[
            pl.BlockSpec((row_block, 128), lambda r, s: (s[1] + r, 0)),
            block,
            pl.BlockSpec((2, planes, row_block, lanes), here),
            *(pl.BlockSpec((min(x.shape[0], 5 - at), planes, row_block, lanes), held) for at, x in zip((0, 3), received)),
            block,
        ],
        out_specs=[block] + [pl.BlockSpec((3, planes, row_block, lanes), sent)] * returns,
    )
    out = pl.pallas_call(
        functools.partial(border_kernel, coeffs, returns, lanes),
        grid_spec=grid_spec,
        out_shape=[jax.ShapeDtypeStruct(acc.shape, jnp.float32)]
        + [jax.ShapeDtypeStruct((3, planes, size, lanes), jnp.float32)] * returns,
        input_output_aliases={4 + len(received): 0},
        compiler_params=params(),
        cost_estimate=heavy if returns else small,
        name="border_part",
    )(flags, step, comp, vel, *received, acc)
    return out


def first_kernel(coeffs, lanes, flag_ref, step_ref, comp_ref, vel_ref, comp_near, vel_near, out_ref):
    local_kernel(coeffs, lanes, step_ref, comp_ref, vel_ref, out_ref)
    border_kernel(coeffs, False, lanes, flag_ref, step_ref, comp_ref, vel_ref, comp_near, vel_near, out_ref, out_ref)


def first_part(flags, coeffs, step, comp, vel, comp_near, vel_near):
    fields, planes, rows, lanes = comp.shape
    at = lambda r, s: (0, 0, r, 0)
    block = pl.BlockSpec((fields, planes, row_block, lanes), at)
    two = pl.BlockSpec((2, planes, row_block, lanes), at)
    grid_spec = pltpu.PrefetchScalarGridSpec(
        num_scalar_prefetch=1,
        grid=(rows // row_block,),
        in_specs=[pl.BlockSpec((row_block, 128), lambda r, s: (r, 0)), block, block, block, two],
        out_specs=block,
    )
    return pl.pallas_call(
        functools.partial(first_kernel, coeffs, lanes),
        grid_spec=grid_spec,
        out_shape=jax.ShapeDtypeStruct(comp.shape, jnp.float32),
        compiler_params=params(),
        cost_estimate=small,
        name="first_part",
    )(flags, step, comp, vel, comp_near, vel_near)


def add_kernel(first, row, row_unit, lane_unit, place_ref, part_ref, acc_ref, out_ref, parts, sums, sems):
    fields, planes, size, lanes = part_ref.shape
    rows = pl.ds(pl.multiple_of(place_ref[0] * row_unit + row, row_block), size)
    columns = pl.ds(pl.multiple_of(place_ref[0] * lane_unit, 128), lanes)
    box = (pl.ds(first, planes), rows, columns)
    loads, stores = [], []
    for f in range(fields):
        loads.append(
            (
                pltpu.make_async_copy(part_ref.at[f], parts.at[f], sems.at[0, f]),
                pltpu.make_async_copy(acc_ref.at[(f, *box)], sums.at[f], sems.at[1, f]),
            )
        )
        stores.append(pltpu.make_async_copy(parts.at[f], out_ref.at[(f, *box)], sems.at[2, f]))
    for pair in loads:
        for load in pair:
            load.start()
    for f in range(fields):
        for load in loads[f]:
            load.wait()
        parts[f] = parts[f] + sums[f]
        stores[f].start()
    for store in stores:
        store.wait()


def add_part(first, row, row_unit, lane_unit, place, part, acc):
    here = pl.BlockSpec(memory_space=pltpu.HBM)
    return pl.pallas_call(
        functools.partial(add_kernel, first, row, row_unit, lane_unit),
        in_specs=[pl.BlockSpec(memory_space=pltpu.SMEM), pl.BlockSpec(memory_space=pl.ANY), here],
        out_specs=here,
        out_shape=jax.ShapeDtypeStruct(acc.shape, jnp.float32),
        input_output_aliases={2: 0},
        scratch_shapes=[pltpu.VMEM(part.shape, jnp.float32)] * 2
        + [pltpu.SemaphoreType.DMA((3, part.shape[0]))],
        compiler_params=pltpu.CompilerParams(vmem_limit_bytes=24 * 1024 * 1024),
        cost_estimate=small,
        name="add_part",
    )(place, part, acc)


def shares(total, unit):
    flat = [w for share in share_weights for w in share]
    ends = [unit * round(total // unit * sum(flat[:k]) / sum(flat)) for k in range(len(flat) + 1)]
    cuts, k = [], 0
    for share in share_weights:
        own = [(a, b - a) for a, b in zip(ends[k:], ends[k + 1 : k + 1 + len(share)]) if b > a]
        cuts.append((ends[k], ends[k + len(share)] - ends[k], own))
        k += len(share)
    return [cut for cut in cuts if cut[1]]


def shards(conformation, velocity):
    planes, rows, lanes = conformation.shape[1:]
    groups, slabs = lax.axis_size("yz"), lax.axis_size("gx")
    me, slab = lax.axis_index("yz"), lax.axis_index("gx")
    odd = (slab % 2).astype(jnp.int32)
    count = rows * groups
    columns = lanes // groups
    spacing = math.pi / (count - 1)
    coeffs = tuple(c / spacing for c in stencil_coeffs)
    half = rows // 2
    wall_cuts = shares(planes, 1)
    border_cuts = shares(half, row_block)
    near = [(i, i ^ 1) for i in range(slabs)]
    far = [(i, (i + 1 if i % 2 else i - 1) % slabs) for i in range(slabs)]

    def along_yz(x, by):
        return lax.ppermute(x, "yz", [(i, (i + by) % groups) for i in range(groups)])

    beside = [lax.ppermute(x, "gx", near) for x in (conformation, velocity)]
    walls, borders = [], []
    for k in range(len(share_weights)):
        places, boxes = [], []
        for plane, n_planes, _ in wall_cuts[k : k + 1]:
            places += [(me + g) % groups for g in range(1, groups)]
            boxes += [(plane, n_planes, 0, 0, rows, columns, columns)] * (groups - 1)
        for row, n_rows, _ in border_cuts[k : k + 1]:
            places.append(odd)
            boxes.append((0, planes, row, half, n_rows, 0, lanes))
        packed = [
            pack(place.astype(jnp.int32).reshape(1), [box], k == 0 and box[-2] > 0, conformation, velocity)[0] for place, box in zip(places, boxes)
        ]
        if k < len(wall_cuts):
            walls.append([along_yz(packed[g - 1], g) for g in range(1, groups)][::-1])
        if k < len(border_cuts):
            borders.append(lax.ppermute(packed[-1], "gx", far))

    index = jnp.arange(count, dtype=jnp.int32)
    points = index % rows * groups + (index // rows + me) % groups
    theta = math.pi * points.astype(jnp.float32) / (count - 1)
    step_size = courant * spacing * (jnp.sin(theta) + spacing)
    cheb = step_size[:, None] * cheb_matrix(count, points)
    high = lax.reduce_precision(cheb, 8, 7)
    low = lax.reduce_precision(cheb - high, 8, 7)
    matrix = jnp.concatenate([high, high, low], axis=1).astype(jnp.bfloat16)
    step = jnp.broadcast_to(step_size[:rows, None], (rows, 128))

    acc = first_part((1 - odd).reshape(1), coeffs, step, conformation, velocity, *beside)
    place = me.astype(jnp.int32).reshape(1)
    returned = []
    for k in range(len(share_weights)):
        wall_own = wall_cuts[k][2] if k < len(wall_cuts) else []
        border_own = border_cuts[k][2] if k < len(border_cuts) else []
        for j in range(max(len(wall_own), len(border_own))):
            if j < len(wall_own):
                at, size = wall_own[j]
                acc, back = wall_part(
                    at, at - wall_cuts[k][0], size, place, conformation, velocity, walls[k], matrix, acc
                )
                for g, b in enumerate(back, 1):
                    source = ((me - g) % groups).astype(jnp.int32).reshape(1)
                    returned.append((at, 0, 0, columns, source, along_yz(b, g)))
            if j < len(border_own):
                at, size = border_own[j]
                far_flags = jnp.stack([odd, ((1 - odd) * half + at) // row_block])
                acc, back = border_part(
                    True, at - border_cuts[k][0], size, far_flags, coeffs, step, conformation, velocity, [borders[k]], acc
                )
                returned.append((0, at, half, 0, odd.reshape(1), lax.ppermute(back, "gx", far)))
    for first, row, row_unit, lane_unit, source, part in returned:
        acc = add_part(first, row, row_unit, lane_unit, source, part, acc)
    return acc


def solution(mesh):
    in_specs = (P(None, "gx", "yz", None), P(None, "gx", "yz", None))
    out_specs = P(None, "gx", "yz", None)
    return jax.shard_map(shards, mesh=mesh, in_specs=in_specs, out_specs=out_specs, check_vma=False)
```

```python
import functools
import math

import jax
import jax.numpy as jnp
from jax import lax
from jax.experimental import pallas as pl
from jax.experimental.pallas import tpu as pltpu
from jax.sharding import PartitionSpec as P

stencil_coeffs = (0.8, -0.2, 4.0 / 105.0, -1.0 / 280.0)
width = 4
extensibility = 10.0
relax_rate = 1.0 / 0.04
courant = 0.5
row_block = 8
share_weights = ((3,), (8, 1))
vmem_bytes = 56 * 1024 * 1024


def cheb_matrix(count, points):
    last = count - 1
    half_step = math.pi / (2.0 * last)
    weights = jnp.where((points == 0) | (points == last), 2.0, 1.0).astype(jnp.float32)
    same = points[:, None] == points[None, :]
    sums = (points[:, None] + points[None, :]).astype(jnp.float32) * half_step
    diffs = (points[:, None] - points[None, :]).astype(jnp.float32) * half_step
    signs = (1 - 2 * ((points[:, None] + points[None, :]) % 2)).astype(jnp.float32)
    apart = -2.0 * jnp.sin(sums) * jnp.sin(diffs)
    safe = jnp.where(same, 1.0, apart)
    offdiag = jnp.where(same, 0.0, weights[:, None] / weights[None, :] * signs / safe)
    return offdiag - jnp.diag(jnp.sum(offdiag, axis=1))


small = pl.CostEstimate(flops=1024, bytes_accessed=1024, transcendentals=0)
heavy = pl.CostEstimate(flops=100000000000, bytes_accessed=1024, transcendentals=0)


def params():
    return pltpu.CompilerParams(vmem_limit_bytes=vmem_bytes)


def x_terms(u, c_xx, c_xy, sums):
    term_xx = 2.0 * sums[3] * c_xx - u * sums[0]
    term_xy = sums[3] * c_xy + sums[4] * c_xx - u * sums[1]
    term_yy = 2.0 * sums[4] * c_xy - u * sums[2]
    return term_xx, term_xy, term_yy


def from_after(planes, i, coeffs):
    return sum(coeffs[k - 1] * planes[i + k - width] for k in range(width - i, width + 1))


def from_before(planes, i, coeffs):
    return -sum(coeffs[k - 1] * planes[width + i - k] for k in range(i + 1, width + 1))


def inside(planes, i, coeffs):
    total = None
    for k in range(1, width):
        for at, sign in ((i + k, 1.0), (i - k, -1.0)):
            if 0 <= at < width:
                term = (sign * coeffs[k - 1]) * planes[at]
                total = term if total is None else total + term
    return total


def local_kernel(coeffs, lanes, step_ref, comp_ref, vel_ref, out_ref):
    step = step_ref[:, 0:1]
    for i in range(width):
        comp = [comp_ref[f, i] for f in range(3)]
        along_z = []
        for f in range(3):
            total = None
            for k in range(1, width + 1):
                ahead = pltpu.roll(comp[f], lanes - k, 1)
                behind = pltpu.roll(comp[f], k, 1)
                term = coeffs[k - 1] * (ahead - behind)
                total = term if total is None else total + term
            along_z.append(total)
        sums = [inside([comp_ref[f, j] for j in range(width)], i, coeffs) for f in range(3)]
        sums += [inside([vel_ref[f, j] for j in range(width)], i, coeffs) for f in range(2)]
        terms = x_terms(vel_ref[0, i], comp[0], comp[1], sums)
        peterlin = (extensibility - 2.0) / (extensibility - comp[0] - comp[2])
        rest = (1.0, 0.0, 1.0)
        w = vel_ref[2, i]
        for f in range(3):
            relax = relax_rate * (peterlin * comp[f] - rest[f])
            out_ref[f, i] = comp[f] + step * (terms[f] - w * along_z[f] - relax)


def pack_kernel(boxes, direct, place_ref, comp_ref, vel_ref, *refs):
    outs, held, sems = refs[: len(boxes)], refs[: len(boxes)] if direct else refs[len(boxes) : -1], refs[-1]
    loads, stores = [], []
    for j, (plane, n_planes, row, row_unit, n_rows, lane_unit, n_lanes) in enumerate(boxes):
        rows = pl.ds(pl.multiple_of(place_ref[j] * row_unit + row, row_block), n_rows)
        lanes = pl.ds(pl.multiple_of(place_ref[j] * lane_unit, 128), n_lanes)
        for source, first, fields in ((comp_ref, 0, 3), (vel_ref, 3, 2)):
            for f in range(fields):
                k, to = len(loads), first + f
                planes = pl.ds(plane, n_planes)
                loads.append(pltpu.make_async_copy(source.at[f, planes, rows, lanes], held[j].at[to], sems.at[0, k]))
                if not direct:
                    stores.append(pltpu.make_async_copy(held[j].at[to], outs[j].at[to], sems.at[1, k]))
    for load in loads:
        load.start()
    for k, load in enumerate(loads):
        load.wait()
        if not direct:
            stores[k].start()
    for store in stores:
        store.wait()


def pack(places, boxes, direct, comp, vel):
    here = pl.BlockSpec(memory_space=pltpu.HBM)
    shapes = [(5, planes, rows, lanes) for _, planes, _, _, rows, _, lanes in boxes]
    return pl.pallas_call(
        functools.partial(pack_kernel, boxes, direct),
        in_specs=[pl.BlockSpec(memory_space=pltpu.SMEM), here, here],
        out_specs=[pl.BlockSpec(memory_space=pltpu.VMEM) if direct else here] * len(boxes),
        out_shape=[pltpu.VMEM(shape, jnp.float32) if direct else jax.ShapeDtypeStruct(shape, jnp.float32) for shape in shapes],
        scratch_shapes=[pltpu.VMEM(shape, jnp.float32) for shape in shapes if not direct]
        + [pltpu.SemaphoreType.DMA((2, 5 * len(boxes)))],
        compiler_params=params(),
        cost_estimate=small,
        name="pack",
    )(places, comp, vel)


def wall_kernel(groups, rows, *refs):
    comp_ref, vel_ref = refs[1:3]
    received = refs[3 : 2 + groups]
    matrix_ref, acc_ref = refs[2 + groups : 4 + groups]
    out_ref = refs[4 + groups]
    back = refs[5 + groups :]
    matrix = matrix_ref[...]
    fields, slopes = [], []
    for f in range(5):
        own = comp_ref[f, 0] if f < 3 else vel_ref[f - 3, 0]
        column = jnp.concatenate([own] + [r[f, 0] for r in received], axis=0)
        high = column.astype(jnp.bfloat16)
        low = (column - high.astype(jnp.float32)).astype(jnp.bfloat16)
        stacked = jnp.concatenate([high, low, high], axis=0)
        slopes.append(jnp.dot(matrix, stacked, preferred_element_type=jnp.float32))
        fields.append(column)
    c_xy, c_yy, v = fields[1], fields[2], fields[4]
    terms = (
        2.0 * slopes[3] * c_xy - v * slopes[0],
        slopes[3] * c_yy + slopes[4] * c_xy - v * slopes[1],
        2.0 * slopes[4] * c_yy - v * slopes[2],
    )
    for f in range(3):
        out_ref[f, 0] = acc_ref[f, 0] + terms[f][0:rows]
        for g in range(1, groups):
            back[g - 1][f, 0] = terms[f][g * rows : (g + 1) * rows]


def wall_part(first, skip, planes, place, comp, vel, received, matrix, acc):
    groups = len(received) + 1
    rows, lanes = comp.shape[2:]
    columns = lanes // groups
    tile = min(columns, 256)
    tiles = columns // tile
    own = lambda p, i, s: (0, first + p, 0, s[0] * tiles + i)
    own_block = pl.BlockSpec((3, 1, rows, tile), own)
    held = lambda p, i, s: (0, skip + p, 0, i)
    sent = lambda p, i, s: (0, p, 0, i)
    grid_spec = pltpu.PrefetchScalarGridSpec(
        num_scalar_prefetch=1,
        grid=(planes, tiles),
        in_specs=[own_block, pl.BlockSpec((2, 1, rows, tile), own)]
        + [pl.BlockSpec((5, 1, rows, tile), held)] * (groups - 1)
        + [pl.BlockSpec(matrix.shape, lambda p, i, s: (0, 0)), own_block],
        out_specs=[own_block] + [pl.BlockSpec((3, 1, rows, tile), sent)] * (groups - 1),
    )
    count = rows * groups
    shapes = [jax.ShapeDtypeStruct(acc.shape, jnp.float32)]
    shapes += [jax.ShapeDtypeStruct((3, planes, rows, columns), jnp.float32)] * (groups - 1)
    out = pl.pallas_call(
        functools.partial(wall_kernel, groups, rows),
        grid_spec=grid_spec,
        out_shape=shapes,
        input_output_aliases={3 + groups: 0},
        compiler_params=params(),
        cost_estimate=heavy,
        name="wall_part",
    )(place, comp, vel, *received, matrix, acc)
    return out[0], out[1:]


def border_kernel(coeffs, returns, lanes, flag_ref, step_ref, comp_ref, vel_ref, *refs):
    received, acc_ref, out_ref, back_ref = (refs[:1], *refs[1:]) if returns else (refs[:2], *refs[2:], None)
    tile = min(lanes, 256)

    def run(after):
        step = step_ref[:, 0:1]
        for at in range(0, lanes, tile):
            here = slice(at, at + tile)
            own = [[(comp_ref[f, i, :, here] if f < 3 else vel_ref[f - 3, i, :, here]) for i in range(width)] for f in range(5)]
            fields = [(received[0], f) for f in range(5)] if returns else [(received[f // 3], f % 3) for f in range(5)]
            other = [[r[f, i, :, here] for i in range(width)] for r, f in fields]
            to_mine, to_theirs = (from_after, from_before) if after else (from_before, from_after)
            for i in range(width):
                mine = [to_mine(other[f], i, coeffs) for f in range(5)]
                terms = x_terms(own[3][i], own[0][i], own[1][i], mine)
                for f in range(3):
                    out_ref[f, i, :, here] = acc_ref[f, i, :, here] + step * terms[f]
                if returns:
                    theirs = [to_theirs(own[f], i, coeffs) for f in range(5)]
                    returned = x_terms(other[3][i], other[0][i], other[1][i], theirs)
                    for f in range(3):
                        back_ref[f, i, :, here] = step * returned[f]

    pl.when(flag_ref[0] == 1)(lambda: run(True))
    pl.when(flag_ref[0] == 0)(lambda: run(False))


def border_part(returns, skip, size, flags, coeffs, step, comp, vel, received, acc):
    planes, lanes = comp.shape[1], comp.shape[3]
    here = lambda r, s: (0, 0, s[1] + r, 0)
    block = pl.BlockSpec((3, planes, row_block, lanes), here)
    held = lambda r, s: (0, 0, skip // row_block + r, 0)
    sent = lambda r, s: (0, 0, r, 0)
    grid_spec = pltpu.PrefetchScalarGridSpec(
        num_scalar_prefetch=1,
        grid=(size // row_block,),
        in_specs=[
            pl.BlockSpec((row_block, 128), lambda r, s: (s[1] + r, 0)),
            block,
            pl.BlockSpec((2, planes, row_block, lanes), here),
            *(pl.BlockSpec((min(x.shape[0], 5 - at), planes, row_block, lanes), held) for at, x in zip((0, 3), received)),
            block,
        ],
        out_specs=[block] + [pl.BlockSpec((3, planes, row_block, lanes), sent)] * returns,
    )
    out = pl.pallas_call(
        functools.partial(border_kernel, coeffs, returns, lanes),
        grid_spec=grid_spec,
        out_shape=[jax.ShapeDtypeStruct(acc.shape, jnp.float32)]
        + [jax.ShapeDtypeStruct((3, planes, size, lanes), jnp.float32)] * returns,
        input_output_aliases={4 + len(received): 0},
        compiler_params=params(),
        cost_estimate=heavy if returns else small,
        name="border_part",
    )(flags, step, comp, vel, *received, acc)
    return out


def first_kernel(coeffs, lanes, flag_ref, step_ref, comp_ref, vel_ref, comp_near, vel_near, out_ref):
    local_kernel(coeffs, lanes, step_ref, comp_ref, vel_ref, out_ref)
    border_kernel(coeffs, False, lanes, flag_ref, step_ref, comp_ref, vel_ref, comp_near, vel_near, out_ref, out_ref)


def first_part(flags, coeffs, step, comp, vel, comp_near, vel_near):
    fields, planes, rows, lanes = comp.shape
    at = lambda r, s: (0, 0, r, 0)
    block = pl.BlockSpec((fields, planes, row_block, lanes), at)
    two = pl.BlockSpec((2, planes, row_block, lanes), at)
    grid_spec = pltpu.PrefetchScalarGridSpec(
        num_scalar_prefetch=1,
        grid=(rows // row_block,),
        in_specs=[pl.BlockSpec((row_block, 128), lambda r, s: (r, 0)), block, block, block, two],
        out_specs=block,
    )
    return pl.pallas_call(
        functools.partial(first_kernel, coeffs, lanes),
        grid_spec=grid_spec,
        out_shape=jax.ShapeDtypeStruct(comp.shape, jnp.float32),
        compiler_params=params(),
        cost_estimate=small,
        name="first_part",
    )(flags, step, comp, vel, comp_near, vel_near)


def add_kernel(first, row, row_unit, lane_unit, place_ref, part_ref, acc_ref, out_ref, parts, sums, sems):
    fields, planes, size, lanes = part_ref.shape
    rows = pl.ds(pl.multiple_of(place_ref[0] * row_unit + row, row_block), size)
    columns = pl.ds(pl.multiple_of(place_ref[0] * lane_unit, 128), lanes)
    box = (pl.ds(first, planes), rows, columns)
    loads, stores = [], []
    for f in range(fields):
        loads.append(
            (
                pltpu.make_async_copy(part_ref.at[f], parts.at[f], sems.at[0, f]),
                pltpu.make_async_copy(acc_ref.at[(f, *box)], sums.at[f], sems.at[1, f]),
            )
        )
        stores.append(pltpu.make_async_copy(parts.at[f], out_ref.at[(f, *box)], sems.at[2, f]))
    for pair in loads:
        for load in pair:
            load.start()
    for f in range(fields):
        for load in loads[f]:
            load.wait()
        parts[f] = parts[f] + sums[f]
        stores[f].start()
    for store in stores:
        store.wait()


def add_part(first, row, row_unit, lane_unit, place, part, acc):
    here = pl.BlockSpec(memory_space=pltpu.HBM)
    return pl.pallas_call(
        functools.partial(add_kernel, first, row, row_unit, lane_unit),
        in_specs=[pl.BlockSpec(memory_space=pltpu.SMEM), pl.BlockSpec(memory_space=pl.ANY), here],
        out_specs=here,
        out_shape=jax.ShapeDtypeStruct(acc.shape, jnp.float32),
        input_output_aliases={2: 0},
        scratch_shapes=[pltpu.VMEM(part.shape, jnp.float32)] * 2
        + [pltpu.SemaphoreType.DMA((3, part.shape[0]))],
        compiler_params=pltpu.CompilerParams(vmem_limit_bytes=24 * 1024 * 1024),
        cost_estimate=small,
        name="add_part",
    )(place, part, acc)


def shares(total, unit):
    flat = [w for share in share_weights for w in share]
    ends = [unit * round(total // unit * sum(flat[:k]) / sum(flat)) for k in range(len(flat) + 1)]
    cuts, k = [], 0
    for share in share_weights:
        own = [(a, b - a) for a, b in zip(ends[k:], ends[k + 1 : k + 1 + len(share)]) if b > a]
        cuts.append((ends[k], ends[k + len(share)] - ends[k], own))
        k += len(share)
    return [cut for cut in cuts if cut[1]]


def shards(conformation, velocity):
    planes, rows, lanes = conformation.shape[1:]
    groups, slabs = lax.axis_size("yz"), lax.axis_size("gx")
    me, slab = lax.axis_index("yz"), lax.axis_index("gx")
    odd = (slab % 2).astype(jnp.int32)
    count = rows * groups
    columns = lanes // groups
    spacing = math.pi / (count - 1)
    coeffs = tuple(c / spacing for c in stencil_coeffs)
    half = rows // 2
    wall_cuts = shares(planes, 1)
    border_cuts = shares(half, row_block)
    near = [(i, i ^ 1) for i in range(slabs)]
    far = [(i, (i + 1 if i % 2 else i - 1) % slabs) for i in range(slabs)]

    def along_yz(x, by):
        return lax.ppermute(x, "yz", [(i, (i + by) % groups) for i in range(groups)])

    beside = [lax.ppermute(x, "gx", near) for x in (conformation, velocity)]
    walls, borders = [], []
    for k in range(len(share_weights)):
        places, boxes = [], []
        for plane, n_planes, _ in wall_cuts[k : k + 1]:
            places += [(me + g) % groups for g in range(1, groups)]
            boxes += [(plane, n_planes, 0, 0, rows, columns, columns)] * (groups - 1)
        for row, n_rows, _ in border_cuts[k : k + 1]:
            places.append(odd)
            boxes.append((0, planes, row, half, n_rows, 0, lanes))
        packed = [
            pack(place.astype(jnp.int32).reshape(1), [box], k == 0 and box[-2] > 0, conformation, velocity)[0] for place, box in zip(places, boxes)
        ]
        if k < len(wall_cuts):
            walls.append([along_yz(packed[g - 1], g) for g in range(1, groups)][::-1])
        if k < len(border_cuts):
            borders.append(lax.ppermute(packed[-1], "gx", far))

    index = jnp.arange(count, dtype=jnp.int32)
    points = index % rows * groups + (index // rows + me) % groups
    theta = math.pi * points.astype(jnp.float32) / (count - 1)
    step_size = courant * spacing * (jnp.sin(theta) + spacing)
    cheb = step_size[:, None] * cheb_matrix(count, points)
    high = lax.reduce_precision(cheb, 8, 7)
    low = lax.reduce_precision(cheb - high, 8, 7)
    matrix = jnp.concatenate([high, high, low], axis=1).astype(jnp.bfloat16)
    step = jnp.broadcast_to(step_size[:rows, None], (rows, 128))

    acc = first_part((1 - odd).reshape(1), coeffs, step, conformation, velocity, *beside)
    place = me.astype(jnp.int32).reshape(1)
    returned = []
    for k in range(len(share_weights)):
        wall_own = wall_cuts[k][2] if k < len(wall_cuts) else []
        border_own = border_cuts[k][2] if k < len(border_cuts) else []
        for j in range(max(len(wall_own), len(border_own))):
            if j < len(wall_own):
                at, size = wall_own[j]
                acc, back = wall_part(
                    at, at - wall_cuts[k][0], size, place, conformation, velocity, walls[k], matrix, acc
                )
                for g, b in enumerate(back, 1):
                    source = ((me - g) % groups).astype(jnp.int32).reshape(1)
                    returned.append((at, 0, 0, columns, source, along_yz(b, g)))
            if j < len(border_own):
                at, size = border_own[j]
                far_flags = jnp.stack([odd, ((1 - odd) * half + at) // row_block])
                acc, back = border_part(
                    True, at - border_cuts[k][0], size, far_flags, coeffs, step, conformation, velocity, [borders[k]], acc
                )
                returned.append((0, at, half, 0, odd.reshape(1), lax.ppermute(back, "gx", far)))
    for first, row, row_unit, lane_unit, source, part in returned:
        acc = add_part(first, row, row_unit, lane_unit, source, part, acc)
    return acc


def solution(mesh):
    in_specs = (P(None, "gx", "yz", None), P(None, "gx", "yz", None))
    out_specs = P(None, "gx", "yz", None)
    return jax.shard_map(shards, mesh=mesh, in_specs=in_specs, out_specs=out_specs, check_vma=False)
```
